512 devices in a mesh: ctx: 64 (over y, z), head: 8 (over x, core).
Axes of the slice: x: 4, y: 4, z: 16, core: 2. Of those that a mesh axis runs over, the one named last changes fastest.
Arguments:
- queries: bfloat16 [16384, 4096], P('ctx', 'head'), may hold values from -144 to 144
- keys: bfloat16 [16384, 1024], P('ctx', 'head'), may hold values from -6 to 6
- values: bfloat16 [16384, 1024], P('ctx', 'head'), may hold values from -6 to 6
- block_ids: int32 [16384], P('ctx'), may hold values from 0 to 1023, as said below
- out_weight: bfloat16 [4096, 4096], P('head'), may hold values from -0.09375 to 0.09375
Outputs:
- mixed: bfloat16 [16384, 4096], P('ctx', 'head')
The draws below stay inside these ranges and needn't reach their ends.
Inputs may be any that keep to these rules, and one draw needn't show every extreme that they name: `block_ids`: block numbers never fall along the sequence; each number of 0 to 1023 names 1 to 32 tokens, and one names exactly 32.
All inputs are finite; a program needn't handle non-finite values.
Results may differ from the reference program's by a relative error of at most 0.02.
Values may be sent and summed in bfloat16 or wider, within the bound.
No kernel may reach another device: no remote copies, remote signals or barrier semaphores. Data moves between devices by JAX's collectives and lax.ppermute only.
A program may use at most 64 MiB of HBM per device.

```python
import jax
import jax.numpy as jnp
from jax import lax

D = 4096
QUERY_HEADS = 32
KEY_VALUE_HEADS = 8
HEAD_SIZE = 128
TOK_DEV = 256
SEQUENCE_TOKENS = 16384
FRAMES = 1024


def shared_keys(key):
    return jax.random.truncated_normal(key, -6.0, 6.0, (SEQUENCE_TOKENS, KEY_VALUE_HEADS * HEAD_SIZE), jnp.float32)


def edge_positions():
    return jnp.arange(1, SEQUENCE_TOKENS // TOK_DEV, dtype=jnp.int32) * TOK_DEV


def draw_block_ids(key, part):
    key = jax.random.fold_in(key, 5)
    first_key, second_key = jax.random.split(key)
    frame_index = jnp.arange(FRAMES, dtype=jnp.int32)
    offsets = jax.random.randint(first_key, (FRAMES,), 1, 16, dtype=jnp.int32)
    longest = jax.random.randint(second_key, (), 1, FRAMES - 2, dtype=jnp.int32)
    offsets = jnp.where(frame_index == longest, 0, offsets)
    offsets = jnp.where(frame_index == longest + 1, 16, offsets)
    starts = frame_index[1:] * 16 + offsets[1:]
    start_marks = jnp.zeros((SEQUENCE_TOKENS,), jnp.int32).at[starts].add(1)
    return jnp.cumsum(start_marks).astype(jnp.int32)


def draw_keys(key, part):
    base_offset = shared_keys(key)
    return base_offset.astype(jnp.bfloat16)


def draw_queries(key, part):
    own_key = jax.random.fold_in(key, 7)
    base_offset = shared_keys(key)
    query_group = QUERY_HEADS // KEY_VALUE_HEADS
    edges = edge_positions()
    edge_count = edges.shape[0]
    fresh_rows = 2.5 * jax.random.truncated_normal(own_key, -6.0, 6.0, (SEQUENCE_TOKENS, QUERY_HEADS * HEAD_SIZE), jnp.float32)
    edge_strength = jnp.full((edge_count,), 12.0, jnp.float32)
    edge_keys = base_offset[edges].reshape(edge_count, KEY_VALUE_HEADS, 1, HEAD_SIZE) * edge_strength[:, None, None, None]
    edge_rows = jnp.broadcast_to(edge_keys, (edge_count, KEY_VALUE_HEADS, query_group, HEAD_SIZE)).reshape(edge_count, QUERY_HEADS * HEAD_SIZE)
    fresh_rows = fresh_rows.at[edges - 1].set(edge_rows)
    return jnp.clip(fresh_rows, -144.0, 144.0).astype(jnp.bfloat16)


def shard_levels(key, extent, cuts, low, high):
    def one(position, parts):
        draws = jax.random.uniform(jax.random.fold_in(jax.random.fold_in(key, 6), position), (parts,), jnp.float32, low / len(cuts), high / len(cuts))
        return jnp.repeat(jnp.exp(draws), extent[position] // parts).reshape((-1,) + (1,) * (len(extent) - position - 1))

    gain = one(*cuts[0])
    for cut in cuts[1:]:
        gain = gain * one(*cut)
    return gain


def centred(stream_key, shape, scale, limit, pieces=(), kind=jnp.bfloat16):
    level = shard_levels(stream_key, shape, pieces, -0.22, 0.18) if pieces else 1.0
    entries = jax.random.normal(stream_key, shape, jnp.float32) * scale * level
    return jnp.minimum(jnp.maximum(entries, -limit), limit).astype(kind)


def setup_inputs(seed: int = 0) -> dict:
    seeds = jax.random.split(jax.random.key(seed), 6)
    return {
        "queries": draw_queries(jax.random.fold_in(seeds[5], 71), 0),
        "keys": draw_keys(jax.random.fold_in(seeds[5], 71), 0),
        "values": centred(seeds[2], (SEQUENCE_TOKENS, KEY_VALUE_HEADS * HEAD_SIZE), 1.0, 6.0, ((0, 64), (1, 8))),
        "block_ids": draw_block_ids(jax.random.fold_in(seeds[5], 71), 0),
        "out_weight": centred(seeds[4], (QUERY_HEADS * HEAD_SIZE, D), (QUERY_HEADS * HEAD_SIZE) ** -0.5, 0.09375, ((0, 8),)),
    }


def reference(queries, keys, values, block_ids, out_weight):
    query_group = QUERY_HEADS // KEY_VALUE_HEADS
    rows_per_block = min(128, SEQUENCE_TOKENS)
    scale = HEAD_SIZE ** -0.5
    heads_of_keys = keys.reshape(SEQUENCE_TOKENS, KEY_VALUE_HEADS, HEAD_SIZE).astype(jnp.float32)
    heads_of_values = values.reshape(SEQUENCE_TOKENS, KEY_VALUE_HEADS, HEAD_SIZE).astype(jnp.float32)

    def one_block(start):
        rows_of_queries = lax.dynamic_slice_in_dim(queries, start, rows_per_block, 0)
        heads_of_queries = rows_of_queries.reshape(rows_per_block, KEY_VALUE_HEADS, query_group, HEAD_SIZE).astype(jnp.float32)
        query_ids = lax.dynamic_slice_in_dim(block_ids, start, rows_per_block, 0)
        scores = jnp.einsum("tkgd,pkd->kgtp", heads_of_queries, heads_of_keys) * scale
        visible = block_ids[None, :] <= query_ids[:, None]
        scores = jnp.where(visible, scores, -1e30)
        rowmax = jnp.max(scores, axis=-1, keepdims=True)
        expo = jnp.where(visible, jnp.exp(scores - rowmax), 0.0)
        totals = jnp.sum(expo, axis=-1)
        weights = expo.astype(jnp.bfloat16)
        summed = jnp.einsum("kgtp,pkd->kgtd", weights.astype(jnp.float32), heads_of_values)
        attended = summed / totals[..., None]
        attended = jnp.transpose(attended, (2, 0, 1, 3)).reshape(rows_per_block, QUERY_HEADS * HEAD_SIZE)
        return attended.astype(jnp.bfloat16)

    starts = (jnp.arange(SEQUENCE_TOKENS // rows_per_block) * rows_per_block).astype(jnp.int32)
    attended = lax.map(one_block, starts).reshape(SEQUENCE_TOKENS, QUERY_HEADS * HEAD_SIZE)
    return jnp.dot(attended, out_weight, preferred_element_type=jnp.float32).astype(jnp.bfloat16)
```

```python
import functools

import jax
import jax.numpy as jnp
import numpy as np
from jax import lax
from jax.experimental import pallas as pl
from jax.experimental.pallas import tpu as pltpu
from jax.sharding import Mesh
from jax.sharding import PartitionSpec as P

HEAD = 128
GROUP = 4
TOK = 256
LOG_SCALE = float(128**-0.5 * np.log2(np.e))
HIDDEN = -1e30
FLOOR = -1e29
ROWS = TOK * 2 + 16
QROWS = TOK + 16
OROWS = GROUP * HEAD + 16
VROWS = HEAD + 16
TILE = 4 * TOK
WIDTH = GROUP * HEAD
F32, BF16 = jnp.float32, jnp.bfloat16
NX, NY, NZ = 4, 4, 16


def ring_place(d, z):
    return ((z // 4 - d) % NY) * NZ + z


def ring_step(step):
    return [
        (ring_place(d, (z + step) % NZ), ring_place(d, z)) for d in range(4) for z in range(NZ)
    ]


def ring_groups():
    return [
        [i * NZ + ((i + d) % 4) * 4 + zl for i in range(4)] for d in range(4) for zl in range(4)
    ]


def schedule():
    table = np.zeros((NY * NZ, 32), np.int32)
    for y in range(NY):
        for z in range(NZ):
            zh, zl = divmod(z, 4)
            d = (zh - y) % 4
            full = [(q, i) for q in range(4) for i in range(q)]
            row = table[y * NZ + z]
            for q in range(4):
                quad = (q + d) % 4
                if quad < zh:
                    full.append((q, q))
                elif quad == zh:
                    row[1] = q
                after = q * NZ + z + 1
                if zl == 3 and after < NY * NZ:
                    i, rest = divmod(after, NZ)
                    if (i + d) % 4 == rest // 4:
                        row[2:5] = 1, q, i
            row[0] = len(full)
            for n, (q, i) in enumerate(full):
                row[8 + n] = q
                row[20 + n] = i
    return table


def dot(a, b, dims):
    return lax.dot_general(a, b, (dims, ((), ())), preferred_element_type=F32)


def attend_kernel(
    info, q_ref, own, ahead, behind, far_low, far_high, out_ref,
    k_buf, v_buf, s0, s1, top, acc, row_max, ids,
):
    sides = (own, ahead, behind)
    for i in range(4):
        for n in range(4):
            if n < 3:
                block = sides[n].at[i]
            else:
                block = (far_low if i < 2 else far_high).at[i % 2]
            k_buf[i, n * TOK : (n + 1) * TOK, :] = block[0:TOK, :]
            v_buf[i, 0:HEAD, n * TOK : (n + 1) * TOK] = block[TOK : 2 * TOK, :].T
        v_buf[i, HEAD:VROWS, :] = jnp.ones((16, TILE), BF16)
    acc[...] = jnp.zeros_like(acc)
    row_max[...] = jnp.full_like(row_max, FLOOR)
    scores = (s0, s1)
    parts = TILE // TOK

    def query(q, h):
        return q_ref[q, 0:TOK, h * HEAD : (h + 1) * HEAD]

    def score_part(q, i, h, c):
        return dot(k_buf[i, c * TOK : (c + 1) * TOK, :], query(q, h), ((1,), (1,)))

    def fold(s):
        return jnp.max(s.reshape(TOK // 8, 8, TOK), axis=0)

    best = None
    for c in range(parts):
        s = score_part(info[8], info[20], 0, c)
        s0[c * TOK : (c + 1) * TOK, :] = s
        best = fold(s) if best is None else jnp.maximum(best, fold(s))
    top[...] = best

    def tile(n, carry):
        q, i = info[8 + n], info[20 + n]
        after = jnp.minimum(n + 1, info[0] - 1)
        q_after, i_after = info[8 + after], info[20 + after]
        for h in range(GROUP):
            now, later = scores[h % 2], scores[(h + 1) % 2]
            q_n, i_n, h_n = (q, i, h + 1) if h < GROUP - 1 else (q_after, i_after, 0)
            old = row_max[q, h : h + 1, :]
            new = jnp.maximum(old, jnp.max(top[...], axis=0, keepdims=True))
            factor = jnp.exp2((old - new) * LOG_SCALE)
            row_max[q, h : h + 1, :] = new
            best = None
            total = acc[q, h] * factor
            for c in range(parts):
                rows = slice(c * TOK, (c + 1) * TOK)
                s = score_part(q_n, i_n, h_n, c)
                later[rows, :] = s
                best = fold(s) if best is None else jnp.maximum(best, fold(s))
                weights = jnp.exp2((now[rows, :] - new) * LOG_SCALE).astype(BF16)
                total = total + dot(v_buf[i, :, rows], weights, ((1,), (0,)))
            acc[q, h] = total
            top[...] = best
        return carry

    lax.fori_loop(0, info[0], tile, 0)

    def masked(q, i, first, size):
        q_ids = (
            q_ref[q, TOK : TOK + 16, 0:TOK].astype(F32) * 32.0
            + q_ref[q, TOK : TOK + 16, TOK : 2 * TOK].astype(F32)
        )[0:1, :]
        hidden = jnp.where(
            jnp.concatenate([ids[0:size, :]] * 2, axis=1) <= q_ids, 0.0, HIDDEN
        )
        for h in range(GROUP):
            s = dot(k_buf[i, first : first + size, :], query(q, h), ((1,), (1,)))
            s = jnp.where(hidden < 0.0, HIDDEN, s)
            old = row_max[q, h : h + 1, :]
            new = jnp.maximum(old, jnp.max(s, axis=0, keepdims=True))
            factor = jnp.exp2((old - new) * LOG_SCALE)
            row_max[q, h : h + 1, :] = new
            weights = jnp.exp2((s - new) * LOG_SCALE).astype(BF16)
            acc[q, h] = acc[q, h] * factor + dot(
                v_buf[i, :, first : first + size], weights, ((1,), (0,))
            )

    def spread_ids(block, at):
        rows = block[2 * TOK : 2 * TOK + 16, :].astype(F32)
        for half in range(2):
            line = rows[half : half + 1, :] * 32.0 + rows[half + 2 : half + 3, :]
            ids[at + half * 128 : at + half * 128 + 128, :] = jnp.broadcast_to(line, (128, 128)).T

    mq = info[1]
    for n in range(3):
        spread_ids(sides[n].at[mq], n * TOK)

    @pl.when(mq < 2)
    def _():
        spread_ids(far_low.at[jnp.minimum(mq, 1)], 3 * TOK)

    @pl.when(mq >= 2)
    def _():
        spread_ids(far_high.at[jnp.maximum(mq - 2, 0)], 3 * TOK)

    masked(mq, mq, 0, TILE)

    @pl.when(info[2] == 1)
    def _():
        spread_ids(ahead.at[info[4]], 0)
        masked(info[3], info[4], TOK, TOK)

    for q in range(4):
        sums = []
        for h in range(GROUP):
            total = jnp.maximum(acc[q, h, HEAD : HEAD + 1, :], 0.5)
            out_ref[q, h * HEAD : (h + 1) * HEAD, :] = (
                acc[q, h, 0:HEAD, :] * (1.0 / total)
            ).astype(BF16)
            sums.append(row_max[q, h : h + 1, :] * LOG_SCALE + jnp.log2(total))
        log_sum = jnp.concatenate(sums, axis=0)
        high = log_sum.astype(BF16).astype(F32)
        mid = (log_sum - high).astype(BF16).astype(F32)
        low = log_sum - high - mid
        out_ref[q, GROUP * HEAD : OROWS, :] = jnp.concatenate(
            [high, mid, low, jnp.zeros_like(low)], axis=0
        ).astype(BF16)


def attend(info, q, own, ahead, behind, far_low, far_high):
    vmem = pl.BlockSpec(memory_space=pltpu.VMEM)
    return pl.pallas_call(
        attend_kernel,
        out_shape=jax.ShapeDtypeStruct((4, OROWS, TOK), BF16),
        in_specs=[pl.BlockSpec(memory_space=pltpu.SMEM)] + [vmem] * 6,
        out_specs=vmem,
        scratch_shapes=[
            pltpu.VMEM((4, TILE, HEAD), BF16),
            pltpu.VMEM((4, VROWS, TILE), BF16),
            pltpu.VMEM((TILE, TOK), F32),
            pltpu.VMEM((TILE, TOK), F32),
            pltpu.VMEM((8, TOK), F32),
            pltpu.VMEM((4, GROUP, VROWS, TOK), F32),
            pltpu.VMEM((4, 8, TOK), F32),
            pltpu.VMEM((TILE, 128), F32),
        ],
        compiler_params=pltpu.CompilerParams(vmem_limit_bytes=40 * 2**20),
        name="attend",
    )(info, q, own, ahead, behind, far_low, far_high)


def combine_kernel(parts, out_ref):
    logs = []
    for y in range(NY):
        tail = parts[y, GROUP * HEAD : OROWS, :].astype(F32)
        logs.append(tail[0:4] + tail[4:8] + tail[8:12])
    best = functools.reduce(jnp.maximum, logs)
    shares = [jnp.exp2(l - best) for l in logs]
    whole = 1.0 / functools.reduce(jnp.add, shares)
    for h in range(GROUP):
        rows = slice(h * HEAD, (h + 1) * HEAD)
        total = None
        for y in range(NY):
            part = parts[y, rows, :].astype(F32) * (shares[y] * whole)[h : h + 1, :]
            total = part if total is None else total + part
        out_ref[:, rows] = total.T.astype(BF16)


def combine(parts):
    vmem = pl.BlockSpec(memory_space=pltpu.VMEM)
    return pl.pallas_call(
        combine_kernel,
        out_shape=jax.ShapeDtypeStruct((TOK, GROUP * HEAD), BF16),
        in_specs=[vmem],
        out_specs=vmem,
        compiler_params=pltpu.CompilerParams(vmem_limit_bytes=16 * 2**20),
        name="combine",
    )(parts)


def pack_kernel(core, weight, out, sems):
    copies = [
        pltpu.make_async_copy(
            weight.at[:, pl.ds(pl.multiple_of((2 * x + 1 - core[0]) * WIDTH, WIDTH), WIDTH)],
            out.at[x],
            sems.at[x],
        )
        for x in range(NX)
    ]
    for copy in copies:
        copy.start()
    for copy in copies:
        copy.wait()


def pack(core, weight):
    anywhere = pl.BlockSpec(memory_space=pl.ANY)
    return pl.pallas_call(
        pack_kernel,
        out_shape=jax.ShapeDtypeStruct((NX, WIDTH, WIDTH), BF16),
        in_specs=[pl.BlockSpec(memory_space=pltpu.SMEM), anywhere],
        out_specs=anywhere,
        scratch_shapes=[pltpu.SemaphoreType.DMA((NX,))],
        name="pack",
    )(core, weight)


def project_kernel(core, both, own_weight, other_weight, out_ref):
    mine, other = both[core[0]], both[1 - core[0]]
    out_ref[0] = (
        dot(mine, own_weight[...], ((1,), (0,))) + dot(other, other_weight[0], ((1,), (0,)))
    ).astype(BF16)


def project(core, both, own_weight, other_weight):
    return pl.pallas_call(
        project_kernel,
        grid_spec=pltpu.PrefetchScalarGridSpec(
            num_scalar_prefetch=1,
            grid=(NX,),
            in_specs=[
                pl.BlockSpec((2, TOK, WIDTH), lambda x, core: (0, 0, 0)),
                pl.BlockSpec((WIDTH, WIDTH), lambda x, core: (0, 2 * x + core[0])),
                pl.BlockSpec((1, WIDTH, WIDTH), lambda x, core: (x, 0, 0)),
            ],
            out_specs=pl.BlockSpec((1, TOK, WIDTH), lambda x, core: (x, 0, 0)),
        ),
        out_shape=jax.ShapeDtypeStruct((NX, TOK, WIDTH), BF16),
        compiler_params=pltpu.CompilerParams(vmem_limit_bytes=16 * 2**20),
        name="project",
    )(core, both, own_weight, other_weight)


def split_ids(block_ids):
    return (block_ids // 32).astype(BF16), (block_ids % 32).astype(BF16)


def local(queries, keys, values, block_ids, out_weight):
    ctx = ("y", "z")
    high, low = split_ids(block_ids)
    info = lax.dynamic_index_in_dim(
        jnp.asarray(schedule()), lax.axis_index(ctx), 0, keepdims=False
    )
    core = lax.axis_index("core").reshape(1)

    q_ids = jnp.zeros((16, GROUP * HEAD), BF16).at[0].set(jnp.concatenate([high, low]))
    q_all = lax.all_gather(jnp.concatenate([queries, q_ids], axis=0), "y", axis=0)
    id_rows = jnp.concatenate([high, low]).reshape(4, 128)
    block = jnp.concatenate([keys, values, id_rows, jnp.zeros((12, 128), BF16)], axis=0)
    own = lax.all_gather(block, ctx, axis=0, axis_index_groups=ring_groups())
    ahead = lax.ppermute(own, ctx, ring_step(1))
    behind = lax.ppermute(own, ctx, ring_step(-1))
    far_low = lax.ppermute(own[0:2], ctx, ring_step(2))
    far_high = lax.ppermute(own[2:4], ctx, ring_step(-2))

    weight, own = lax.optimization_barrier((out_weight, own))
    other_weight = lax.ppermute(pack(core, weight), "core", [(0, 1), (1, 0)])

    partial = attend(info, q_all, own, ahead, behind, far_low, far_high)
    partial = lax.all_to_all(partial, "y", 0, 0, tiled=True)
    both = lax.all_gather(combine(partial), "core", axis=0)
    share = project(core, both, out_weight, other_weight)
    shares = lax.all_to_all(share, "x", 0, 0, tiled=True)
    return jnp.sum(shares.astype(F32), axis=0).astype(BF16)


def solution(mesh):
    grid = Mesh(mesh.devices.reshape(NY, NZ, NX, 2), ("y", "z", "x", "core"))
    ctx, head = ("y", "z"), ("x", "core")
    return jax.shard_map(
        local,
        mesh=grid,
        in_specs=(P(ctx, head), P(ctx, head), P(ctx, head), P(ctx), P(head, None)),
        out_specs=P(ctx, head),
        check_vma=False,
    )
```

```python
import functools

import jax
import jax.numpy as jnp
import numpy as np
from jax import lax
from jax.experimental import pallas as pl
from jax.experimental.pallas import tpu as pltpu
from jax.sharding import Mesh
from jax.sharding import PartitionSpec as P

HEAD = 128
GROUP = 4
TOK = 256
LOG_SCALE = float(128**-0.5 * np.log2(np.e))
HIDDEN = -1e30
FLOOR = -1e29
ROWS = TOK * 2 + 16
QROWS = TOK + 16
OROWS = GROUP * HEAD + 16
VROWS = HEAD + 16
WIDTH = GROUP * HEAD
F32, BF16 = jnp.float32, jnp.bfloat16
NX, NY, NZ = 4, 4, 16


def ring_place(d, z):
    return ((z // 4 - d) % NY) * NZ + z


def ring_step(step):
    return [
        (ring_place(d, (z + step) % NZ), ring_place(d, z)) for d in range(4) for z in range(NZ)
    ]


def ring_groups():
    return [
        [i * NZ + ((i + d) % 4) * 4 + zl for i in range(4)] for d in range(4) for zl in range(4)
    ]


def run_on():
    table = np.zeros((NY * NZ, 8), np.int32)
    for y in range(NY - 1):
        table[y * NZ + NZ - 1, 0:3] = 1, y, y + 1
    return table


def dot(a, b, dims):
    return lax.dot_general(a, b, (dims, ((), ())), preferred_element_type=F32)


def attend_kernel(kinds, first, last, info, q_ref, *refs):
    n_blocks = 1 + max(operand for kind in kinds for operand, _ in kind)
    blocks, refs = refs[:n_blocks], refs[n_blocks:]
    if first:
        acc_in = max_in = None
    else:
        acc_in, max_in, *refs = refs
    if last:
        out_ref, acc, row_max, *refs = refs
    else:
        acc, row_max, *refs = refs
    v_buf, even, odd, top, ids = refs
    scores = (even, odd)

    def key_block(n, i):
        operand, index = kinds[n][i]
        return blocks[operand].at[index]

    for n in range(len(kinds)):
        for i in range(4):
            block = key_block(n, i)
            v_buf[n, i, 0:HEAD, :] = block[TOK : 2 * TOK, :].T
            v_buf[n, i, HEAD:VROWS, :] = jnp.ones((16, TOK), BF16)
            rows = block[2 * TOK : 2 * TOK + 16, :].astype(F32)
            for half in range(2):
                line = rows[half : half + 1, :] * 32.0 + rows[half + 2 : half + 3, :]
                ids[n, i, half * 128 : half * 128 + 128, :] = jnp.broadcast_to(line, (128, 128)).T

    def query(q, h):
        return q_ref[q, 0:TOK, pl.ds(pl.multiple_of(h * HEAD, HEAD), HEAD)]

    def query_ids(q):
        tail = q_ref[q, TOK : TOK + 16, :].astype(F32)
        return (tail[:, 0:TOK] * 32.0 + tail[:, TOK : 2 * TOK])[0:1, :]

    def hide(s, q, n, i):
        seen = jnp.concatenate([ids[n, i], ids[n, i]], axis=1) <= query_ids(q)
        return jnp.where(seen, s, HIDDEN)

    def score(q, h, n, i):
        s = dot(key_block(n, i)[0:TOK, :], query(q, h), ((1,), (1,)))
        return hide(s, q, n, i) if i == q else s

    def fold(s):
        return jnp.max(s.reshape(TOK // 8, 8, TOK), axis=0)

    parts = [[(n, i) for i in range(q + 1) for n in range(len(kinds))] for q in range(4)]

    def score_into(q, h, at, best):
        s = score(q, h, *parts[q][at])
        scores[q % 2][at * TOK : (at + 1) * TOK, :] = s
        return fold(s) if best is None else jnp.maximum(best, fold(s))

    best = None
    for at in range(len(parts[0])):
        best = score_into(0, 0, at, best)
    top[...] = best

    def head(h, carry):
        for q in range(4):
            q_next, h_next = (q + 1, h) if q < 3 else (0, jnp.minimum(h + 1, GROUP - 1))
            peak = jnp.max(top[...], axis=0, keepdims=True)
            if first:
                new = jnp.maximum(peak, FLOOR)
                total = None
            else:
                old = max_in[q, h]
                new = jnp.maximum(old, peak)
                total = acc_in[q, h] * jnp.exp2((old - new) * LOG_SCALE)
            row_max[q, h] = new
            best = None
            here, there = len(parts[q]), len(parts[q_next])
            done = 0
            for at, (n, i) in enumerate(parts[q]):
                until = (at + 1) * there // here
                for other in range(done, until):
                    best = score_into(q_next, h_next, other, best)
                done = until
                weights = jnp.exp2(
                    (scores[q % 2][at * TOK : (at + 1) * TOK, :] - new) * LOG_SCALE
                ).astype(BF16)
                part = dot(v_buf[n, i], weights, ((1,), (0,)))
                total = part if total is None else total + part
            acc[q, h] = total
            top[...] = best
        return carry

    lax.fori_loop(0, GROUP, head, 0)

    if kinds == AHEAD_BEHIND:
        @pl.when(info[0] == 1)
        def _():
            q, i = info[1], info[2]
            block = blocks[0].at[i]
            seen = jnp.concatenate([ids[0, i], ids[0, i]], axis=1) <= query_ids(q)
            for h in range(GROUP):
                s = dot(block[0:TOK, :], query(q, h), ((1,), (1,)))
                s = jnp.where(seen, s, HIDDEN)
                old = row_max[q, h]
                new = jnp.maximum(old, jnp.max(s, axis=0, keepdims=True))
                weights = jnp.exp2((s - new) * LOG_SCALE).astype(BF16)
                acc[q, h] = acc[q, h] * jnp.exp2((old - new) * LOG_SCALE) + dot(
                    v_buf[0, i], weights, ((1,), (0,))
                )
                row_max[q, h] = new

    if last:
        for q in range(4):
            sums = []
            for h in range(GROUP):
                total = jnp.maximum(acc[q, h, HEAD : HEAD + 1, :], 0.5)
                out_ref[q, h * HEAD : (h + 1) * HEAD, :] = (
                    acc[q, h, 0:HEAD, :] * (1.0 / total)
                ).astype(BF16)
                sums.append(row_max[q, h] * LOG_SCALE + jnp.log2(total))
            log_sum = jnp.concatenate(sums, axis=0)
            high = log_sum.astype(BF16).astype(F32)
            mid = (log_sum - high).astype(BF16).astype(F32)
            low = log_sum - high - mid
            out_ref[q, GROUP * HEAD : OROWS, :] = jnp.concatenate(
                [high, mid, low, jnp.zeros_like(low)], axis=0
            ).astype(BF16)


OWN = (((0, 0), (0, 1), (0, 2), (0, 3)),)
AHEAD_BEHIND = (((0, 0), (0, 1), (0, 2), (0, 3)), ((1, 0), (1, 1), (1, 2), (1, 3)))
FAR = (((0, 0), (0, 1), (1, 0), (1, 1)),)


def attend(kinds, first, last, info, q, blocks, state):
    vmem = pl.BlockSpec(memory_space=pltpu.VMEM)
    n = len(kinds)
    acc = jax.ShapeDtypeStruct((4, GROUP, VROWS, TOK), F32)
    row_max = jax.ShapeDtypeStruct((4, GROUP, 1, TOK), F32)
    running = [pltpu.VMEM(acc.shape, F32), pltpu.VMEM(row_max.shape, F32)]
    scores = 10 * n * 4 * TOK * TOK
    return pl.pallas_call(
        functools.partial(attend_kernel, kinds, first, last),
        out_shape=jax.ShapeDtypeStruct((4, OROWS, TOK), BF16) if last else (acc, row_max),
        in_specs=[pl.BlockSpec(memory_space=pltpu.SMEM)] + [vmem] * (1 + len(blocks) + len(state)),
        out_specs=vmem if last else (vmem, vmem),
        scratch_shapes=(running if last else [])
        + [
            pltpu.VMEM((n, 4, VROWS, TOK), BF16),
            pltpu.VMEM((3 * n * TOK, TOK), F32),
            pltpu.VMEM((4 * n * TOK, TOK), F32),
            pltpu.VMEM((8, TOK), F32),
            pltpu.VMEM((n, 4, TOK, 128), F32),
        ],
        compiler_params=pltpu.CompilerParams(vmem_limit_bytes=32 * 2**20),
        cost_estimate=pl.CostEstimate(
            flops=scores * 8 * HEAD, transcendentals=scores, bytes_accessed=6 * 2**20
        ),
        name="attend",
    )(info, q, *blocks, *state)


def combine_kernel(parts, out_ref):
    logs = []
    for y in range(NY):
        tail = parts[y, GROUP * HEAD : OROWS, :].astype(F32)
        logs.append(tail[0:4] + tail[4:8] + tail[8:12])
    best = functools.reduce(jnp.maximum, logs)
    shares = [jnp.exp2(l - best) for l in logs]
    whole = 1.0 / functools.reduce(jnp.add, shares)
    for h in range(GROUP):
        rows = slice(h * HEAD, (h + 1) * HEAD)
        total = None
        for y in range(NY):
            part = parts[y, rows, :].astype(F32) * (shares[y] * whole)[h : h + 1, :]
            total = part if total is None else total + part
        out_ref[:, rows] = total.T.astype(BF16)


def combine(parts):
    vmem = pl.BlockSpec(memory_space=pltpu.VMEM)
    return pl.pallas_call(
        combine_kernel,
        out_shape=jax.ShapeDtypeStruct((TOK, GROUP * HEAD), BF16),
        in_specs=[vmem],
        out_specs=vmem,
        compiler_params=pltpu.CompilerParams(vmem_limit_bytes=16 * 2**20),
        name="combine",
    )(parts)


def pack_kernel(core, weight, out):
    out[0] = weight[...]


def pack(core, weight):
    return pl.pallas_call(
        pack_kernel,
        grid_spec=pltpu.PrefetchScalarGridSpec(
            num_scalar_prefetch=1,
            grid=(NX,),
            in_specs=[pl.BlockSpec((WIDTH, WIDTH), lambda x, core: (0, 2 * x + 1 - core[0]))],
            out_specs=pl.BlockSpec((1, WIDTH, WIDTH), lambda x, core: (x, 0, 0)),
        ),
        out_shape=jax.ShapeDtypeStruct((NX, WIDTH, WIDTH), BF16),
        compiler_params=pltpu.CompilerParams(vmem_limit_bytes=16 * 2**20),
        name="pack",
    )(core, weight)


def project_kernel(core, both, own_weight, other_weight, out_ref):
    mine, other = both[core[0]], both[1 - core[0]]
    out_ref[0] = (
        dot(mine, own_weight[...], ((1,), (0,))) + dot(other, other_weight[0], ((1,), (0,)))
    ).astype(BF16)


def project(core, both, own_weight, other_weight):
    return pl.pallas_call(
        project_kernel,
        grid_spec=pltpu.PrefetchScalarGridSpec(
            num_scalar_prefetch=1,
            grid=(NX,),
            in_specs=[
                pl.BlockSpec((2, TOK, WIDTH), lambda x, core: (0, 0, 0)),
                pl.BlockSpec((WIDTH, WIDTH), lambda x, core: (0, 2 * x + core[0])),
                pl.BlockSpec((1, WIDTH, WIDTH), lambda x, core: (x, 0, 0)),
            ],
            out_specs=pl.BlockSpec((1, TOK, WIDTH), lambda x, core: (x, 0, 0)),
        ),
        out_shape=jax.ShapeDtypeStruct((NX, TOK, WIDTH), BF16),
        compiler_params=pltpu.CompilerParams(vmem_limit_bytes=16 * 2**20),
        name="project",
    )(core, both, own_weight, other_weight)


def split_ids(block_ids):
    return (block_ids // 32).astype(BF16), (block_ids % 32).astype(BF16)


def local(queries, keys, values, block_ids, out_weight):
    ctx = ("y", "z")
    high, low = split_ids(block_ids)
    info = lax.dynamic_index_in_dim(
        jnp.asarray(run_on()), lax.axis_index(ctx), 0, keepdims=False
    )
    core = lax.axis_index("core").reshape(1)

    q_ids = jnp.zeros((16, GROUP * HEAD), BF16).at[0].set(jnp.concatenate([high, low]))
    q_all = lax.all_gather(jnp.concatenate([queries, q_ids], axis=0), "y", axis=0)
    id_rows = jnp.concatenate([high, low]).reshape(4, 128)
    block = jnp.concatenate([keys, values, id_rows, jnp.zeros((12, 128), BF16)], axis=0)
    own = lax.all_gather(block, ctx, axis=0, axis_index_groups=ring_groups())
    ahead = lax.ppermute(own, ctx, ring_step(1))
    behind = lax.ppermute(own, ctx, ring_step(-1))
    far_low = lax.ppermute(own[0:2], ctx, ring_step(2))
    far_high = lax.ppermute(own[2:4], ctx, ring_step(-2))

    state = attend(OWN, True, False, info, q_all, [own], ())
    weight, state = lax.optimization_barrier((out_weight, state))
    other_weight = lax.ppermute(pack(core, weight), "core", [(0, 1), (1, 0)])
    state = attend(AHEAD_BEHIND, False, False, info, q_all, [ahead, behind], state)
    partial = attend(FAR, False, True, info, q_all, [far_low, far_high], state)
    partial = lax.all_to_all(partial, "y", 0, 0, tiled=True)
    both = lax.all_gather(combine(partial), "core", axis=0)
    share = project(core, both, out_weight, other_weight)
    shares = lax.all_to_all(share, "x", 0, 0, tiled=True)
    return jnp.sum(shares.astype(F32), axis=0).astype(BF16)


def solution(mesh):
    grid = Mesh(mesh.devices.reshape(NY, NZ, NX, 2), ("y", "z", "x", "core"))
    ctx, head = ("y", "z"), ("x", "core")
    return jax.shard_map(
        local,
        mesh=grid,
        in_specs=(P(ctx, head), P(ctx, head), P(ctx, head), P(ctx), P(head, None)),
        out_specs=P(ctx, head),
        check_vma=False,
    )
```

```python
import functools

import jax
import jax.numpy as jnp
import numpy as np
from jax import lax
from jax.experimental import pallas as pl
from jax.experimental.pallas import tpu as pltpu
from jax.sharding import Mesh
from jax.sharding import PartitionSpec as P

HEAD = 128
GROUP = 4
TOK = 256
LOG_SCALE = float(128**-0.5 * np.log2(np.e))
HIDDEN = -1e30
FLOOR = -1e29
ROWS = TOK * 2 + 16
QROWS = TOK + 16
OROWS = GROUP * HEAD + 16
VROWS = HEAD + 16
WIDTH = GROUP * HEAD
F32, BF16 = jnp.float32, jnp.bfloat16
NX, NY, NZ = 4, 4, 16


def ring_place(d, z):
    return ((z // 4 - d) % NY) * NZ + z


def ring_step(step):
    return [
        (ring_place(d, (z + step) % NZ), ring_place(d, z)) for d in range(4) for z in range(NZ)
    ]


def ring_groups():
    return [
        [i * NZ + ((i + d) % 4) * 4 + zl for i in range(4)] for d in range(4) for zl in range(4)
    ]


def dot(a, b, dims):
    return lax.dot_general(a, b, (dims, ((), ())), preferred_element_type=F32)


def attend_kernel(kinds, first, last, y_ref, z_ref, q_ref, *refs):
    n_blocks = 1 + max(operand for kind in kinds for operand, _ in kind)
    blocks, refs = refs[:n_blocks], refs[n_blocks:]
    if first:
        acc_in = max_in = None
    else:
        acc_in, max_in, *refs = refs
    if last:
        out_ref, acc, row_max, *refs = refs
    else:
        acc, row_max, *refs = refs
    v_buf, even, odd, top, ids = refs
    scores = (even, odd)

    def key_block(n, i):
        operand, index = kinds[n][i]
        return blocks[operand].at[index]

    for n in range(len(kinds)):
        for i in range(4):
            block = key_block(n, i)
            v_buf[n, i, 0:HEAD, :] = block[TOK : 2 * TOK, :].T
            v_buf[n, i, HEAD:VROWS, :] = jnp.ones((16, TOK), BF16)
            rows = block[2 * TOK : 2 * TOK + 16, :].astype(F32)
            for half in range(2):
                line = rows[half : half + 1, :] * 32.0 + rows[half + 2 : half + 3, :]
                ids[n, i, half * 128 : half * 128 + 128, :] = jnp.broadcast_to(line, (128, 128)).T

    def query(q, h):
        return q_ref[q, 0:TOK, pl.ds(pl.multiple_of(h * HEAD, HEAD), HEAD)]

    def query_ids(q):
        tail = q_ref[q, TOK : TOK + 16, :].astype(F32)
        return (tail[:, 0:TOK] * 32.0 + tail[:, TOK : 2 * TOK])[0:1, :]

    def hide(s, q, n, i):
        seen = jnp.concatenate([ids[n, i], ids[n, i]], axis=1) <= query_ids(q)
        return jnp.where(seen, s, HIDDEN)

    def score(q, h, n, i):
        s = dot(key_block(n, i)[0:TOK, :], query(q, h), ((1,), (1,)))
        return hide(s, q, n, i) if i == q else s

    def fold(s):
        return jnp.max(s.reshape(TOK // 8, 8, TOK), axis=0)

    parts = [[(n, i) for i in range(q + 1) for n in range(len(kinds))] for q in range(4)]

    def score_into(q, h, at, best):
        s = score(q, h, *parts[q][at])
        scores[q % 2][at * TOK : (at + 1) * TOK, :] = s
        return fold(s) if best is None else jnp.maximum(best, fold(s))

    best = None
    for at in range(len(parts[0])):
        best = score_into(0, 0, at, best)
    top[...] = best

    def head(h, carry):
        for q in range(4):
            q_next, h_next = (q + 1, h) if q < 3 else (0, jnp.minimum(h + 1, GROUP - 1))
            peak = jnp.max(top[...], axis=0, keepdims=True)
            if first:
                new = jnp.maximum(peak, FLOOR)
                total = None
            else:
                old = max_in[q, h]
                new = jnp.maximum(old, peak)
                total = acc_in[q, h] * jnp.exp2((old - new) * LOG_SCALE)
            row_max[q, h] = new
            best = None
            here, there = len(parts[q]), len(parts[q_next])
            done = 0
            for at, (n, i) in enumerate(parts[q]):
                until = (at + 1) * there // here
                for other in range(done, until):
                    best = score_into(q_next, h_next, other, best)
                done = until
                weights = jnp.exp2(
                    (scores[q % 2][at * TOK : (at + 1) * TOK, :] - new) * LOG_SCALE
                ).astype(BF16)
                part = dot(v_buf[n, i], weights, ((1,), (0,)))
                total = part if total is None else total + part
            acc[q, h] = total
            top[...] = best
        return carry

    lax.fori_loop(0, GROUP, head, 0)

    if kinds == AHEAD_BEHIND:
        @pl.when((z_ref[0] == NZ - 1) & (y_ref[0] < NY - 1))
        def _():
            q, i = y_ref[0], y_ref[0] + 1
            block = blocks[0].at[i]
            seen = jnp.concatenate([ids[0, i], ids[0, i]], axis=1) <= query_ids(q)
            for h in range(GROUP):
                s = dot(block[0:TOK, :], query(q, h), ((1,), (1,)))
                s = jnp.where(seen, s, HIDDEN)
                old = row_max[q, h]
                new = jnp.maximum(old, jnp.max(s, axis=0, keepdims=True))
                weights = jnp.exp2((s - new) * LOG_SCALE).astype(BF16)
                acc[q, h] = acc[q, h] * jnp.exp2((old - new) * LOG_SCALE) + dot(
                    v_buf[0, i], weights, ((1,), (0,))
                )
                row_max[q, h] = new

    if last:
        for q in range(4):
            sums = []
            for h in range(GROUP):
                total = jnp.maximum(acc[q, h, HEAD : HEAD + 1, :], 0.5)
                out_ref[q, h * HEAD : (h + 1) * HEAD, :] = (
                    acc[q, h, 0:HEAD, :] * (1.0 / total)
                ).astype(BF16)
                sums.append(row_max[q, h] * LOG_SCALE + jnp.log2(total))
            log_sum = jnp.concatenate(sums, axis=0)
            high = log_sum.astype(BF16).astype(F32)
            mid = (log_sum - high).astype(BF16).astype(F32)
            low = log_sum - high - mid
            out_ref[q, GROUP * HEAD : OROWS, :] = jnp.concatenate(
                [high, mid, low, jnp.zeros_like(low)], axis=0
            ).astype(BF16)


OWN = FAR = (((0, 0), (0, 1), (0, 2), (0, 3)),)
AHEAD_BEHIND = (((0, 0), (0, 1), (0, 2), (0, 3)), ((1, 0), (1, 1), (1, 2), (1, 3)))


def attend(kinds, first, last, place, q, blocks, state):
    vmem = pl.BlockSpec(memory_space=pltpu.VMEM)
    n = len(kinds)
    acc = jax.ShapeDtypeStruct((4, GROUP, VROWS, TOK), F32)
    row_max = jax.ShapeDtypeStruct((4, GROUP, 1, TOK), F32)
    running = [pltpu.VMEM(acc.shape, F32), pltpu.VMEM(row_max.shape, F32)]
    scores = 10 * n * 4 * TOK * TOK
    return pl.pallas_call(
        functools.partial(attend_kernel, kinds, first, last),
        out_shape=jax.ShapeDtypeStruct((4, OROWS, TOK), BF16) if last else (acc, row_max),
        in_specs=[pl.BlockSpec(memory_space=pltpu.SMEM)] * 2
        + [vmem] * (1 + len(blocks) + len(state)),
        out_specs=vmem if last else (vmem, vmem),
        scratch_shapes=(running if last else [])
        + [
            pltpu.VMEM((n, 4, VROWS, TOK), BF16),
            pltpu.VMEM((3 * n * TOK, TOK), F32),
            pltpu.VMEM((4 * n * TOK, TOK), F32),
            pltpu.VMEM((8, TOK), F32),
            pltpu.VMEM((n, 4, TOK, 128), F32),
        ],
        compiler_params=pltpu.CompilerParams(vmem_limit_bytes=32 * 2**20),
        cost_estimate=pl.CostEstimate(
            flops=scores * 8 * HEAD, transcendentals=scores, bytes_accessed=6 * 2**20
        ),
        name="attend",
    )(*place, q, *blocks, *state)


def combine_kernel(parts, out_ref):
    logs = []
    for y in range(NY):
        tail = parts[y, GROUP * HEAD : OROWS, :].astype(F32)
        logs.append(tail[0:4] + tail[4:8] + tail[8:12])
    best = functools.reduce(jnp.maximum, logs)
    shares = [jnp.exp2(l - best) for l in logs]
    whole = 1.0 / functools.reduce(jnp.add, shares)
    for h in range(GROUP):
        rows = slice(h * HEAD, (h + 1) * HEAD)
        total = None
        for y in range(NY):
            part = parts[y, rows, :].astype(F32) * (shares[y] * whole)[h : h + 1, :]
            total = part if total is None else total + part
        out_ref[:, rows] = total.T.astype(BF16)


def combine(parts):
    vmem = pl.BlockSpec(memory_space=pltpu.VMEM)
    return pl.pallas_call(
        combine_kernel,
        out_shape=jax.ShapeDtypeStruct((TOK, GROUP * HEAD), BF16),
        in_specs=[vmem],
        out_specs=vmem,
        compiler_params=pltpu.CompilerParams(vmem_limit_bytes=16 * 2**20),
        name="combine",
    )(parts)


def pack_kernel(core, weight, out):
    out[0] = weight[...]


def pack(core, weight):
    return pl.pallas_call(
        pack_kernel,
        grid_spec=pltpu.PrefetchScalarGridSpec(
            num_scalar_prefetch=1,
            grid=(NX,),
            in_specs=[pl.BlockSpec((WIDTH, WIDTH), lambda x, core: (0, 2 * x + 1 - core[0]))],
            out_specs=pl.BlockSpec((1, WIDTH, WIDTH), lambda x, core: (x, 0, 0)),
        ),
        out_shape=jax.ShapeDtypeStruct((NX, WIDTH, WIDTH), BF16),
        compiler_params=pltpu.CompilerParams(vmem_limit_bytes=16 * 2**20),
        name="pack",
    )(core, weight)


def project_kernel(core, both, own_weight, other_weight, out_ref):
    mine, other = both[core[0]], both[1 - core[0]]
    out_ref[0] = (
        dot(mine, own_weight[...], ((1,), (0,))) + dot(other, other_weight[0], ((1,), (0,)))
    ).astype(BF16)


def project(core, both, own_weight, other_weight):
    return pl.pallas_call(
        project_kernel,
        grid_spec=pltpu.PrefetchScalarGridSpec(
            num_scalar_prefetch=1,
            grid=(NX,),
            in_specs=[
                pl.BlockSpec((2, TOK, WIDTH), lambda x, core: (0, 0, 0)),
                pl.BlockSpec((WIDTH, WIDTH), lambda x, core: (0, 2 * x + core[0])),
                pl.BlockSpec((1, WIDTH, WIDTH), lambda x, core: (x, 0, 0)),
            ],
            out_specs=pl.BlockSpec((1, TOK, WIDTH), lambda x, core: (x, 0, 0)),
        ),
        out_shape=jax.ShapeDtypeStruct((NX, TOK, WIDTH), BF16),
        compiler_params=pltpu.CompilerParams(vmem_limit_bytes=16 * 2**20),
        name="project",
    )(core, both, own_weight, other_weight)


def stage_kernel(q, k, v, ids, q_out, block_out):
    high = (ids[...] >> 5).astype(F32)
    low = (ids[...] & 31).astype(F32)
    q_out[0:TOK, :] = q[...]
    terms = (high[0:1], high[1:2], low[0:1], low[1:2])
    for n, term in enumerate(terms):
        q_out[TOK:QROWS, n * 128 : (n + 1) * 128] = jnp.broadcast_to(term, (16, 128)).astype(BF16)
    block_out[0:TOK, :] = k[...]
    block_out[TOK : 2 * TOK, :] = v[...]
    block_out[2 * TOK : ROWS, :] = jnp.concatenate(
        [high, low, jnp.zeros((12, 128), F32)], axis=0
    ).astype(BF16)


def stage(q, k, v, ids):
    vmem = pl.BlockSpec(memory_space=pltpu.VMEM)
    return pl.pallas_call(
        stage_kernel,
        out_shape=(
            jax.ShapeDtypeStruct((QROWS, WIDTH), BF16),
            jax.ShapeDtypeStruct((ROWS, HEAD), BF16),
        ),
        in_specs=[vmem] * 4,
        out_specs=(vmem, vmem),
        compiler_params=pltpu.CompilerParams(vmem_limit_bytes=56 * 2**20),
        name="stage",
    )(q, k, v, ids)


def local(queries, keys, values, block_ids, out_weight):
    ctx = ("y", "z")
    place = [lax.axis_index(axis).reshape(1) for axis in ctx]
    core = lax.axis_index("core").reshape(1)

    staged, block = stage(queries, keys, values, block_ids.reshape(2, 128))
    q_all = lax.all_gather(staged, "y", axis=0)
    own = lax.all_gather(block, ctx, axis=0, axis_index_groups=ring_groups())
    ahead = lax.ppermute(own, ctx, ring_step(1))
    behind = lax.ppermute(own, ctx, ring_step(-1))

    state = attend(OWN, True, False, place, q_all, [own], ())
    sent, state = lax.optimization_barrier((own, state))
    far = lax.ppermute(
        sent,
        (*ctx, "core"),
        [(2 * a + c, 2 * b + c) for c in range(2) for a, b in ring_step(2 - 4 * c)],
    )
    state = attend(AHEAD_BEHIND, False, False, place, q_all, [ahead, behind], state)
    partial = attend(FAR, False, True, place, q_all, [far], state)
    weight, partial = lax.optimization_barrier((out_weight, partial))
    other_weight = lax.ppermute(pack(core, weight), "core", [(0, 1), (1, 0)])
    partial = lax.all_to_all(partial, "y", 0, 0, tiled=True)
    both = lax.all_gather(combine(partial), "core", axis=0)
    share = project(core, both, out_weight, other_weight)
    shares = lax.all_to_all(share, "x", 0, 0, tiled=True)
    return jnp.sum(shares.astype(F32), axis=0).astype(BF16)


def solution(mesh):
    grid = Mesh(mesh.devices.reshape(NY, NZ, NX, 2), ("y", "z", "x", "core"))
    ctx, head = ("y", "z"), ("x", "core")
    return jax.shard_map(
        local,
        mesh=grid,
        in_specs=(P(ctx, head), P(ctx, head), P(ctx, head), P(ctx), P(head, None)),
        out_specs=P(ctx, head),
        check_vma=False,
    )
```

```python
import functools

import jax
import jax.numpy as jnp
import numpy as np
from jax import lax
from jax.experimental import pallas as pl
from jax.experimental.pallas import tpu as pltpu
from jax.sharding import Mesh
from jax.sharding import PartitionSpec as P

HEAD = 128
GROUP = 4
TOK = 256
LOG_SCALE = float(128**-0.5 * np.log2(np.e))
HIDDEN = -1e30
FLOOR = -1e29
ROWS = TOK * 2 + 16
QROWS = TOK + 16
OROWS = GROUP * HEAD + 16
VROWS = HEAD + 16
WIDTH = GROUP * HEAD
F32, BF16 = jnp.float32, jnp.bfloat16
NX, NY, NZ = 4, 4, 16


def ring_place(d, z):
    return ((z // 4 - d) % NY) * NZ + z


def ring_step(step):
    return [
        (ring_place(d, (z + step) % NZ), ring_place(d, z)) for d in range(4) for z in range(NZ)
    ]


def ring_groups():
    return [
        [i * NZ + ((i + d) % 4) * 4 + zl for i in range(4)] for d in range(4) for zl in range(4)
    ]


def dot(a, b, dims):
    return lax.dot_general(a, b, (dims, ((), ())), preferred_element_type=F32)


def attend_kernel(steps, first, last, y_ref, z_ref, q_ref, *refs):
    kinds = len(steps)
    blocks, refs = refs[:kinds], refs[kinds:]
    if first:
        acc_in = max_in = None
    else:
        acc_in, max_in, *refs = refs
    if last:
        out_ref, acc, row_max, *refs = refs
    else:
        acc, row_max, *refs = refs
    v_buf, score_1, score_2, score_3, top = refs
    scores = (None, score_1, score_2, score_3)

    def key_block(n, i):
        return blocks[n].at[i]

    for n in range(kinds):
        for i in range(4):
            v_buf[n, i, 0:HEAD, :] = key_block(n, i)[TOK : 2 * TOK, :].T
            v_buf[n, i, HEAD:VROWS, :] = jnp.ones((16, TOK), BF16)

    def query(q, h):
        return q_ref[q, 0:TOK, pl.ds(pl.multiple_of(h * HEAD, HEAD), HEAD)]

    def score(q, h, n, i):
        return dot(key_block(n, i)[0:TOK, :], query(q, h), ((1,), (1,)))

    def fold(s):
        return jnp.max(s.reshape(TOK // 8, 8, TOK), axis=0)

    parts = [[(n, i) for i in range(q) for n in range(kinds)] for q in range(4)]

    def score_into(q, h, at, best):
        s = score(q, h, *parts[q][at])
        scores[q][at * TOK : (at + 1) * TOK, :] = s
        return fold(s) if best is None else jnp.maximum(best, fold(s))

    best = None
    for at in range(len(parts[1])):
        best = score_into(1, 0, at, best)
    top[...] = best

    def head(h, carry):
        for q in range(1, 4):
            q_next, h_next = (q + 1, h) if q < 3 else (1, jnp.minimum(h + 1, GROUP - 1))
            peak = jnp.max(top[...], axis=0, keepdims=True)
            if first:
                new = jnp.maximum(peak, FLOOR)
                total = None
            else:
                old = max_in[q, h]
                new = jnp.maximum(old, peak)
                total = acc_in[q, h] * jnp.exp2((old - new) * LOG_SCALE)
            row_max[q, h] = new
            best = None
            here, there = len(parts[q]), len(parts[q_next])
            done = 0
            for at, (n, i) in enumerate(parts[q]):
                until = (at + 1) * there // here
                for other in range(done, until):
                    best = score_into(q_next, h_next, other, best)
                done = until
                weights = jnp.exp2(
                    (scores[q][at * TOK : (at + 1) * TOK, :] - new) * LOG_SCALE
                ).astype(BF16)
                part = dot(v_buf[n, i], weights, ((1,), (0,)))
                total = part if total is None else total + part
            acc[q, h] = total
            top[...] = best
        return carry

    lax.fori_loop(0, GROUP, head, 0)

    if first:
        acc[0] = jnp.zeros((GROUP, VROWS, TOK), F32)
        row_max[0] = jnp.full((GROUP, 1, TOK), FLOOR, F32)
    else:
        acc[0] = acc_in[0]
        row_max[0] = max_in[0]

    def by_number(n, q, i):
        rows = key_block(n, i)[2 * TOK : 2 * TOK + 16, :].astype(F32)
        key_ids = []
        for half in range(2):
            line = rows[half : half + 1, :] * 32.0 + rows[half + 2 : half + 3, :]
            key_ids.append(jnp.broadcast_to(line, (128, 128)).T)
        key_ids = jnp.concatenate(key_ids, axis=0)
        tail = q_ref[q, TOK : TOK + 16, :].astype(F32)
        query_ids = (tail[:, 0:TOK] * 32.0 + tail[:, TOK : 2 * TOK])[0:1, :]
        seen = jnp.concatenate([key_ids, key_ids], axis=1) <= query_ids
        s = score(q, 0, n, i)
        for h in range(GROUP):
            s_next = score(q, h + 1, n, i) if h + 1 < GROUP else None
            s = jnp.where(seen, s, HIDDEN)
            old = row_max[q, h]
            new = jnp.maximum(old, jnp.max(s, axis=0, keepdims=True))
            weights = jnp.exp2((s - new) * LOG_SCALE).astype(BF16)
            acc[q, h] = acc[q, h] * jnp.exp2((old - new) * LOG_SCALE) + dot(
                v_buf[n, i], weights, ((1,), (0,))
            )
            row_max[q, h] = new
            s = s_next

    y, z = y_ref[0], z_ref[0]
    d = (z // 4 + 4 - y) % 4
    for n, step in enumerate(steps):
        kind = (z + step + 4) % 4
        count = jnp.minimum((z + 5 - kind) // 4, 4)

        def run(t, carry, n=n):
            q = (t + 4 - d) % 4
            by_number(n, q, q)
            return carry

        lax.fori_loop(0, count, run, 0)
        if step == 1:
            @pl.when((z == NZ - 1) & (y < NY - 1))
            def _(n=n):
                by_number(n, y, y + 1)

    if last:
        for q in range(4):
            sums = []
            for h in range(GROUP):
                total = jnp.maximum(acc[q, h, HEAD : HEAD + 1, :], 0.5)
                out_ref[q, h * HEAD : (h + 1) * HEAD, :] = (
                    acc[q, h, 0:HEAD, :] * (1.0 / total)
                ).astype(BF16)
                sums.append(row_max[q, h] * LOG_SCALE + jnp.log2(total))
            log_sum = jnp.concatenate(sums, axis=0)
            high = log_sum.astype(BF16).astype(F32)
            mid = (log_sum - high).astype(BF16).astype(F32)
            low = log_sum - high - mid
            out_ref[q, GROUP * HEAD : OROWS, :] = jnp.concatenate(
                [high, mid, low, jnp.zeros_like(low)], axis=0
            ).astype(BF16)


def attend(steps, first, last, place, q, blocks, state):
    vmem = pl.BlockSpec(memory_space=pltpu.VMEM)
    n = len(steps)
    acc = jax.ShapeDtypeStruct((4, GROUP, VROWS, TOK), F32)
    row_max = jax.ShapeDtypeStruct((4, GROUP, 1, TOK), F32)
    running = [pltpu.VMEM(acc.shape, F32), pltpu.VMEM(row_max.shape, F32)]
    scores = 10 * n * 4 * TOK * TOK
    return pl.pallas_call(
        functools.partial(attend_kernel, steps, first, last),
        out_shape=jax.ShapeDtypeStruct((4, OROWS, TOK), BF16) if last else (acc, row_max),
        in_specs=[pl.BlockSpec(memory_space=pltpu.SMEM)] * 2
        + [vmem] * (1 + len(blocks) + len(state)),
        out_specs=vmem if last else (vmem, vmem),
        input_output_aliases={} if first or last else {3 + n: 0, 4 + n: 1},
        scratch_shapes=(running if last else [])
        + [
            pltpu.VMEM((n, 4, VROWS, TOK), BF16),
            pltpu.VMEM((n * TOK, TOK), F32),
            pltpu.VMEM((2 * n * TOK, TOK), F32),
            pltpu.VMEM((3 * n * TOK, TOK), F32),
            pltpu.VMEM((8, TOK), F32),
        ],
        compiler_params=pltpu.CompilerParams(vmem_limit_bytes=20 * 2**20),
        cost_estimate=pl.CostEstimate(
            flops=scores * 8 * HEAD, transcendentals=scores, bytes_accessed=6 * 2**20
        ),
        name="attend",
    )(*place, q, *blocks, *state)


def combine_kernel(parts, out_ref):
    logs = []
    for y in range(NY):
        tail = parts[y, GROUP * HEAD : OROWS, :].astype(F32)
        logs.append(tail[0:4] + tail[4:8] + tail[8:12])
    best = functools.reduce(jnp.maximum, logs)
    shares = [jnp.exp2(l - best) for l in logs]
    whole = 1.0 / functools.reduce(jnp.add, shares)
    for h in range(GROUP):
        rows = slice(h * HEAD, (h + 1) * HEAD)
        total = None
        for y in range(NY):
            part = parts[y, rows, :].astype(F32) * (shares[y] * whole)[h : h + 1, :]
            total = part if total is None else total + part
        out_ref[:, rows] = total.T.astype(BF16)


def combine(parts):
    vmem = pl.BlockSpec(memory_space=pltpu.VMEM)
    return pl.pallas_call(
        combine_kernel,
        out_shape=jax.ShapeDtypeStruct((TOK, GROUP * HEAD), BF16),
        in_specs=[vmem],
        out_specs=vmem,
        compiler_params=pltpu.CompilerParams(vmem_limit_bytes=16 * 2**20),
        name="combine",
    )(parts)


def pack_kernel(core, weight, out):
    out[0] = weight[...]


def pack(core, weight):
    return pl.pallas_call(
        pack_kernel,
        grid_spec=pltpu.PrefetchScalarGridSpec(
            num_scalar_prefetch=1,
            grid=(NX,),
            in_specs=[pl.BlockSpec((WIDTH, WIDTH), lambda x, core: (0, 2 * x + 1 - core[0]))],
            out_specs=pl.BlockSpec((1, WIDTH, WIDTH), lambda x, core: (x, 0, 0)),
        ),
        out_shape=jax.ShapeDtypeStruct((NX, WIDTH, WIDTH), BF16),
        compiler_params=pltpu.CompilerParams(vmem_limit_bytes=16 * 2**20),
        name="pack",
    )(core, weight)


def project_kernel(core, both, own_weight, other_weight, out_ref):
    mine, other = both[core[0]], both[1 - core[0]]
    out_ref[0] = (
        dot(mine, own_weight[...], ((1,), (0,))) + dot(other, other_weight[0], ((1,), (0,)))
    ).astype(BF16)


def project(core, both, own_weight, other_weight):
    return pl.pallas_call(
        project_kernel,
        grid_spec=pltpu.PrefetchScalarGridSpec(
            num_scalar_prefetch=1,
            grid=(NX,),
            in_specs=[
                pl.BlockSpec((2, TOK, WIDTH), lambda x, core: (0, 0, 0)),
                pl.BlockSpec((WIDTH, WIDTH), lambda x, core: (0, 2 * x + core[0])),
                pl.BlockSpec((1, WIDTH, WIDTH), lambda x, core: (x, 0, 0)),
            ],
            out_specs=pl.BlockSpec((1, TOK, WIDTH), lambda x, core: (x, 0, 0)),
        ),
        out_shape=jax.ShapeDtypeStruct((NX, TOK, WIDTH), BF16),
        compiler_params=pltpu.CompilerParams(vmem_limit_bytes=16 * 2**20),
        name="project",
    )(core, both, own_weight, other_weight)


def stage_kernel(q, k, v, ids, q_out, block_out):
    high = (ids[...] >> 5).astype(F32)
    low = (ids[...] & 31).astype(F32)
    q_out[0:TOK, :] = q[...]
    terms = (high[0:1], high[1:2], low[0:1], low[1:2])
    for n, term in enumerate(terms):
        q_out[TOK:QROWS, n * 128 : (n + 1) * 128] = jnp.broadcast_to(term, (16, 128)).astype(BF16)
    block_out[0:TOK, :] = k[...]
    block_out[TOK : 2 * TOK, :] = v[...]
    block_out[2 * TOK : ROWS, :] = jnp.concatenate(
        [high, low, jnp.zeros((12, 128), F32)], axis=0
    ).astype(BF16)


def stage(q, k, v, ids):
    vmem = pl.BlockSpec(memory_space=pltpu.VMEM)
    return pl.pallas_call(
        stage_kernel,
        out_shape=(
            jax.ShapeDtypeStruct((QROWS, WIDTH), BF16),
            jax.ShapeDtypeStruct((ROWS, HEAD), BF16),
        ),
        in_specs=[vmem] * 4,
        out_specs=(vmem, vmem),
        compiler_params=pltpu.CompilerParams(vmem_limit_bytes=56 * 2**20),
        name="stage",
    )(q, k, v, ids)


def local(queries, keys, values, block_ids, out_weight):
    ctx = ("y", "z")
    place = [lax.axis_index(axis).reshape(1) for axis in ctx]
    core = lax.axis_index("core").reshape(1)

    staged, block = stage(queries, keys, values, block_ids.reshape(2, 128))
    q_all = lax.all_gather(staged, "y", axis=0)
    own = lax.all_gather(block, ctx, axis=0, axis_index_groups=ring_groups())
    ahead = lax.ppermute(own, ctx, ring_step(1))
    behind = lax.ppermute(own, ctx, ring_step(-1))

    state = attend((0,), True, False, place, q_all, [own], ())
    weight, row_max = lax.optimization_barrier((out_weight, state[1]))
    state = (state[0], row_max)
    other_weight = lax.ppermute(pack(core, weight), "core", [(0, 1), (1, 0)])
    far = lax.ppermute(
        jnp.where(core == 0, ahead, behind),
        (*ctx, "core"),
        [(2 * a + c, 2 * b + c) for c in range(2) for a, b in ring_step(1 - 2 * c)],
    )
    state = attend((1, -1), False, False, place, q_all, [ahead, behind], state)
    partial = attend((2,), False, True, place, q_all, [far], state)
    partial = lax.all_to_all(partial, "y", 0, 0, tiled=True)
    both = lax.all_gather(combine(partial), "core", axis=0)
    share = project(core, both, out_weight, other_weight)
    shares = lax.all_to_all(share, "x", 0, 0, tiled=True)
    return jnp.sum(shares.astype(F32), axis=0).astype(BF16)


def solution(mesh):
    grid = Mesh(mesh.devices.reshape(NY, NZ, NX, 2), ("y", "z", "x", "core"))
    ctx, head = ("y", "z"), ("x", "core")
    return jax.shard_map(
        local,
        mesh=grid,
        in_specs=(P(ctx, head), P(ctx, head), P(ctx, head), P(ctx), P(head, None)),
        out_specs=P(ctx, head),
        check_vma=False,
    )
```

```python
import functools

import jax
import jax.numpy as jnp
import numpy as np
from jax import lax
from jax.experimental import pallas as pl
from jax.experimental.pallas import tpu as pltpu
from jax.sharding import Mesh
from jax.sharding import PartitionSpec as P

HEAD = 128
GROUP = 4
TOK = 256
LOG_SCALE = float(128**-0.5 * np.log2(np.e))
HIDDEN = -1e30
FLOOR = -1e29
ROWS = TOK * 2 + 16
QROWS = TOK + 16
OROWS = GROUP * HEAD + 16
VROWS = HEAD + 16
WIDTH = GROUP * HEAD
F32, BF16 = jnp.float32, jnp.bfloat16
NX, NY, NZ = 4, 4, 16


def ring_place(d, z):
    return ((z // 4 - d) % NY) * NZ + z


def ring_step(step):
    return [
        (ring_place(d, (z + step) % NZ), ring_place(d, z)) for d in range(4) for z in range(NZ)
    ]


def ring_groups():
    return [
        [i * NZ + ((i + d) % 4) * 4 + zl for i in range(4)] for d in range(4) for zl in range(4)
    ]


def dot(a, b, dims):
    return lax.dot_general(a, b, (dims, ((), ())), preferred_element_type=F32)


def attend_kernel(steps, first, last, y_ref, z_ref, q_ref, *refs):
    kinds = len(steps)
    blocks, refs = refs[:kinds], refs[kinds:]
    y, z = y_ref[0], z_ref[0]
    d = (z // 4 + 4 - y) % 4
    if first:
        acc_in = max_in = None
    else:
        acc_in, max_in, *refs = refs
    if last:
        out_ref, acc, row_max, *refs = refs
    else:
        acc, row_max, *refs = refs
    v_buf, score_1, score_2, score_3, top = refs
    scores = (None, score_1, score_2, score_3)

    def key_block(n, i):
        return blocks[n].at[i]

    def query_block(q):
        return q_ref.at[(q + 4 - y) % 4]

    for n in range(kinds):
        for i in range(4):
            v_buf[n, i, 0:HEAD, :] = key_block(n, i)[TOK : 2 * TOK, :].T
            v_buf[n, i, HEAD:VROWS, :] = jnp.ones((16, TOK), BF16)

    def query(q, h):
        return query_block(q)[0:TOK, pl.ds(pl.multiple_of(h * HEAD, HEAD), HEAD)]

    def score(q, h, n, i):
        return dot(key_block(n, i)[0:TOK, :], query(q, h), ((1,), (1,)))

    def fold(s):
        return jnp.max(s.reshape(TOK // 8, 8, TOK), axis=0)

    parts = [[(n, i) for i in range(q) for n in range(kinds)] for q in range(4)]

    def score_into(q, h, at, best):
        s = score(q, h, *parts[q][at])
        scores[q][at * TOK : (at + 1) * TOK, :] = s
        return fold(s) if best is None else jnp.maximum(best, fold(s))

    best = None
    for at in range(len(parts[1])):
        best = score_into(1, 0, at, best)
    top[...] = best

    def head(h, carry):
        for q in range(1, 4):
            q_next, h_next = (q + 1, h) if q < 3 else (1, jnp.minimum(h + 1, GROUP - 1))
            peak = jnp.max(top[...], axis=0, keepdims=True)
            if first:
                new = jnp.maximum(peak, FLOOR)
                total = None
            else:
                old = max_in[q, h]
                new = jnp.maximum(old, peak)
                total = acc_in[q, h] * jnp.exp2((old - new) * LOG_SCALE)
            row_max[q, h] = new
            best = None
            here, there = len(parts[q]), len(parts[q_next])
            done = 0
            for at, (n, i) in enumerate(parts[q]):
                until = (at + 1) * there // here
                for other in range(done, until):
                    best = score_into(q_next, h_next, other, best)
                done = until
                weights = jnp.exp2(
                    (scores[q][at * TOK : (at + 1) * TOK, :] - new) * LOG_SCALE
                ).astype(BF16)
                part = dot(v_buf[n, i], weights, ((1,), (0,)))
                total = part if total is None else total + part
            acc[q, h] = total
            top[...] = best
        return carry

    lax.fori_loop(0, GROUP, head, 0)

    if first:
        acc[0] = jnp.zeros((GROUP, VROWS, TOK), F32)
        row_max[0] = jnp.full((GROUP, 1, TOK), FLOOR, F32)
    else:
        acc[0] = acc_in[0]
        row_max[0] = max_in[0]

    def by_number(n, q, i):
        rows = key_block(n, i)[2 * TOK : 2 * TOK + 16, :].astype(F32)
        key_ids = []
        for half in range(2):
            line = rows[half : half + 1, :] * 32.0 + rows[half + 2 : half + 3, :]
            key_ids.append(jnp.broadcast_to(line, (128, 128)).T)
        key_ids = jnp.concatenate(key_ids, axis=0)
        tail = query_block(q)[TOK : TOK + 16, :].astype(F32)
        query_ids = (tail[:, 0:TOK] * 32.0 + tail[:, TOK : 2 * TOK])[0:1, :]
        seen = jnp.concatenate([key_ids, key_ids], axis=1) <= query_ids
        s = score(q, 0, n, i)
        for h in range(GROUP):
            s_next = score(q, h + 1, n, i) if h + 1 < GROUP else None
            s = jnp.where(seen, s, HIDDEN)
            old = row_max[q, h]
            new = jnp.maximum(old, jnp.max(s, axis=0, keepdims=True))
            weights = jnp.exp2((s - new) * LOG_SCALE).astype(BF16)
            acc[q, h] = acc[q, h] * jnp.exp2((old - new) * LOG_SCALE) + dot(
                v_buf[n, i], weights, ((1,), (0,))
            )
            row_max[q, h] = new
            s = s_next

    for n, step in enumerate(steps):
        kind = (z + step + 4) % 4
        count = jnp.minimum((z + 5 - kind) // 4, 4)

        def run(t, carry, n=n):
            q = (t + 4 - d) % 4
            by_number(n, q, q)
            return carry

        lax.fori_loop(0, count, run, 0)
        if step == 1:
            @pl.when((z == NZ - 1) & (y < NY - 1))
            def _(n=n):
                by_number(n, y, y + 1)

    if last:
        for q in range(4):
            sums = []
            for h in range(GROUP):
                total = jnp.maximum(acc[q, h, HEAD : HEAD + 1, :], 0.5)
                out_ref[q, h * HEAD : (h + 1) * HEAD, :] = (
                    acc[q, h, 0:HEAD, :] * (1.0 / total)
                ).astype(BF16)
                sums.append(row_max[q, h] * LOG_SCALE + jnp.log2(total))
            log_sum = jnp.concatenate(sums, axis=0)
            high = log_sum.astype(BF16).astype(F32)
            mid = (log_sum - high).astype(BF16).astype(F32)
            low = log_sum - high - mid
            out_ref[q, GROUP * HEAD : OROWS, :] = jnp.concatenate(
                [high, mid, low, jnp.zeros_like(low)], axis=0
            ).astype(BF16)


def attend(steps, first, last, place, q, blocks, state):
    vmem = pl.BlockSpec(memory_space=pltpu.VMEM)
    n = len(steps)
    acc = jax.ShapeDtypeStruct((4, GROUP, VROWS, TOK), F32)
    row_max = jax.ShapeDtypeStruct((4, GROUP, 1, TOK), F32)
    running = [pltpu.VMEM(acc.shape, F32), pltpu.VMEM(row_max.shape, F32)]
    scores = 10 * n * 4 * TOK * TOK
    return pl.pallas_call(
        functools.partial(attend_kernel, steps, first, last),
        out_shape=jax.ShapeDtypeStruct((4, OROWS, TOK), BF16) if last else (acc, row_max),
        in_specs=[pl.BlockSpec(memory_space=pltpu.SMEM)] * 2
        + [vmem] * (1 + len(blocks) + len(state)),
        out_specs=vmem if last else (vmem, vmem),
        input_output_aliases={} if first or last else {3 + n: 0, 4 + n: 1},
        scratch_shapes=(running if last else [])
        + [
            pltpu.VMEM((n, 4, VROWS, TOK), BF16),
            pltpu.VMEM((n * TOK, TOK), F32),
            pltpu.VMEM((2 * n * TOK, TOK), F32),
            pltpu.VMEM((3 * n * TOK, TOK), F32),
            pltpu.VMEM((8, TOK), F32),
        ],
        compiler_params=pltpu.CompilerParams(vmem_limit_bytes=20 * 2**20),
        cost_estimate=pl.CostEstimate(
            flops=scores * 8 * HEAD, transcendentals=scores, bytes_accessed=6 * 2**20
        ),
        name="attend",
    )(*place, q, *blocks, *state)


def combine_kernel(parts, out_ref):
    logs = []
    for y in range(NY):
        tail = parts[y, GROUP * HEAD : OROWS, :].astype(F32)
        logs.append(tail[0:4] + tail[4:8] + tail[8:12])
    best = functools.reduce(jnp.maximum, logs)
    shares = [jnp.exp2(l - best) for l in logs]
    whole = 1.0 / functools.reduce(jnp.add, shares)
    for h in range(GROUP):
        rows = slice(h * HEAD, (h + 1) * HEAD)
        total = None
        for y in range(NY):
            part = parts[y, rows, :].astype(F32) * (shares[y] * whole)[h : h + 1, :]
            total = part if total is None else total + part
        out_ref[:, rows] = total.T.astype(BF16)


def combine(parts):
    vmem = pl.BlockSpec(memory_space=pltpu.VMEM)
    return pl.pallas_call(
        combine_kernel,
        out_shape=jax.ShapeDtypeStruct((TOK, GROUP * HEAD), BF16),
        in_specs=[vmem],
        out_specs=vmem,
        compiler_params=pltpu.CompilerParams(vmem_limit_bytes=16 * 2**20),
        name="combine",
    )(parts)


def pack_kernel(core, weight, out):
    out[0] = weight[...]


def pack(core, weight):
    return pl.pallas_call(
        pack_kernel,
        grid_spec=pltpu.PrefetchScalarGridSpec(
            num_scalar_prefetch=1,
            grid=(NX,),
            in_specs=[pl.BlockSpec((WIDTH, WIDTH), lambda x, core: (0, 2 * x + 1 - core[0]))],
            out_specs=pl.BlockSpec((1, WIDTH, WIDTH), lambda x, core: (x, 0, 0)),
        ),
        out_shape=jax.ShapeDtypeStruct((NX, WIDTH, WIDTH), BF16),
        compiler_params=pltpu.CompilerParams(vmem_limit_bytes=16 * 2**20),
        name="pack",
    )(core, weight)


def project_kernel(core, both, own_weight, other_weight, out_ref):
    mine, other = both[core[0]], both[1 - core[0]]
    out_ref[0] = (
        dot(mine, own_weight[...], ((1,), (0,))) + dot(other, other_weight[0], ((1,), (0,)))
    ).astype(BF16)


def project(core, both, own_weight, other_weight):
    return pl.pallas_call(
        project_kernel,
        grid_spec=pltpu.PrefetchScalarGridSpec(
            num_scalar_prefetch=1,
            grid=(NX,),
            in_specs=[
                pl.BlockSpec((2, TOK, WIDTH), lambda x, core: (0, 0, 0)),
                pl.BlockSpec((WIDTH, WIDTH), lambda x, core: (0, 2 * x + core[0])),
                pl.BlockSpec((1, WIDTH, WIDTH), lambda x, core: (x, 0, 0)),
            ],
            out_specs=pl.BlockSpec((1, TOK, WIDTH), lambda x, core: (x, 0, 0)),
        ),
        out_shape=jax.ShapeDtypeStruct((NX, TOK, WIDTH), BF16),
        compiler_params=pltpu.CompilerParams(vmem_limit_bytes=16 * 2**20),
        name="project",
    )(core, both, own_weight, other_weight)


def stage_kernel(q, k, v, ids, q_out, block_out):
    high = (ids[...] >> 5).astype(F32)
    low = (ids[...] & 31).astype(F32)
    q_out[0:TOK, :] = q[...]
    terms = (high[0:1], high[1:2], low[0:1], low[1:2])
    for n, term in enumerate(terms):
        q_out[TOK:QROWS, n * 128 : (n + 1) * 128] = jnp.broadcast_to(term, (16, 128)).astype(BF16)
    block_out[0:TOK, :] = k[...]
    block_out[TOK : 2 * TOK, :] = v[...]
    block_out[2 * TOK : ROWS, :] = jnp.concatenate(
        [high, low, jnp.zeros((12, 128), F32)], axis=0
    ).astype(BF16)


def stage(q, k, v, ids):
    vmem = pl.BlockSpec(memory_space=pltpu.VMEM)
    return pl.pallas_call(
        stage_kernel,
        out_shape=(
            jax.ShapeDtypeStruct((QROWS, WIDTH), BF16),
            jax.ShapeDtypeStruct((ROWS, HEAD), BF16),
        ),
        in_specs=[vmem] * 4,
        out_specs=(vmem, vmem),
        compiler_params=pltpu.CompilerParams(vmem_limit_bytes=56 * 2**20),
        name="stage",
    )(q, k, v, ids)


def local(queries, keys, values, block_ids, out_weight):
    ctx = ("y", "z")
    place = [lax.axis_index(axis).reshape(1) for axis in ctx]
    core = lax.axis_index("core").reshape(1)

    staged, block = stage(queries, keys, values, block_ids.reshape(2, 128))
    q_others = [
        lax.ppermute(staged, "y", [((i + n) % NY, i) for i in range(NY)]) for n in (1, 2, 3)
    ]
    own = lax.all_gather(block, ctx, axis=0, axis_index_groups=ring_groups())
    ahead = lax.ppermute(own, ctx, ring_step(1))
    behind = lax.ppermute(own, ctx, ring_step(-1))

    q_all = jnp.stack([staged, *q_others])
    state = attend((0,), True, False, place, q_all, [own], ())
    weight, row_max = lax.optimization_barrier((out_weight, state[1]))
    state = (state[0], row_max)
    other_weight = lax.ppermute(pack(core, weight), "core", [(0, 1), (1, 0)])
    far = lax.ppermute(
        jnp.where(core == 0, ahead, behind),
        (*ctx, "core"),
        [(2 * a + c, 2 * b + c) for c in range(2) for a, b in ring_step(1 - 2 * c)],
    )
    state = attend((1, -1), False, False, place, q_all, [ahead, behind], state)
    partial = attend((2,), False, True, place, q_all, [far], state)
    partial = lax.all_to_all(partial, "y", 0, 0, tiled=True)
    both = lax.all_gather(combine(partial), "core", axis=0)
    share = project(core, both, out_weight, other_weight)
    shares = lax.all_to_all(share, "x", 0, 0, tiled=True)
    return jnp.sum(shares.astype(F32), axis=0).astype(BF16)


def solution(mesh):
    grid = Mesh(mesh.devices.reshape(NY, NZ, NX, 2), ("y", "z", "x", "core"))
    ctx, head = ("y", "z"), ("x", "core")
    return jax.shard_map(
        local,
        mesh=grid,
        in_specs=(P(ctx, head), P(ctx, head), P(ctx, head), P(ctx), P(head, None)),
        out_specs=P(ctx, head),
        check_vma=False,
    )
```

```python
import functools

import jax
import jax.numpy as jnp
import numpy as np
from jax import lax
from jax.experimental import pallas as pl
from jax.experimental.pallas import tpu as pltpu
from jax.sharding import Mesh
from jax.sharding import PartitionSpec as P

HEAD = 128
GROUP = 4
TOK = 256
LOG_SCALE = float(128**-0.5 * np.log2(np.e))
HIDDEN = -1e30
FLOOR = -1e29
ROWS = TOK * 2 + 16
QROWS = TOK + 16
OROWS = GROUP * HEAD + 16
VROWS = HEAD + 16
WIDTH = GROUP * HEAD
F32, BF16 = jnp.float32, jnp.bfloat16
NX, NY, NZ = 4, 4, 16


def ring_place(d, z):
    return ((z // 4 - d) % NY) * NZ + z


def ring_step(step):
    return [
        (ring_place(d, (z + step) % NZ), ring_place(d, z)) for d in range(4) for z in range(NZ)
    ]


def ring_groups():
    return [
        [i * NZ + ((i + d) % 4) * 4 + zl for i in range(4)] for d in range(4) for zl in range(4)
    ]


def dot(a, b, dims):
    return lax.dot_general(a, b, (dims, ((), ())), preferred_element_type=F32)


def attend_kernel(steps, first, last, y_ref, z_ref, q_ref, *refs):
    kinds = len(steps)
    blocks, refs = refs[:kinds], refs[kinds:]
    y, z = y_ref[0], z_ref[0]
    d = (z // 4 + 4 - y) % 4
    if first:
        acc_in = max_in = None
    else:
        acc_in, max_in, *refs = refs
    if last:
        out_ref, acc, row_max, *refs = refs
    else:
        acc, row_max, *refs = refs
    v_buf, score_1, score_2, score_3, top = refs
    scores = (None, score_1, score_2, score_3)

    def key_block(n, i):
        return blocks[n].at[i]

    def query_block(q):
        return q_ref.at[(q + 4 - y) % 4]

    for n in range(kinds):
        for i in range(4):
            v_buf[n, i, 0:HEAD, :] = key_block(n, i)[TOK : 2 * TOK, :].T
            v_buf[n, i, HEAD:VROWS, :] = jnp.ones((16, TOK), BF16)

    def query(q, h):
        return query_block(q)[0:TOK, pl.ds(pl.multiple_of(h * HEAD, HEAD), HEAD)]

    def score(q, h, n, i):
        return dot(key_block(n, i)[0:TOK, :], query(q, h), ((1,), (1,)))

    def fold(s):
        return jnp.max(s.reshape(TOK // 8, 8, TOK), axis=0)

    parts = [[(n, i) for i in range(q) for n in range(kinds)] for q in range(4)]

    def score_into(q, h, at, best):
        s = score(q, h, *parts[q][at])
        scores[q][at * TOK : (at + 1) * TOK, :] = s
        return fold(s) if best is None else jnp.maximum(best, fold(s))

    best = None
    for at in range(len(parts[1])):
        best = score_into(1, 0, at, best)
    top[...] = best

    def head(h, carry):
        for q in range(1, 4):
            q_next, h_next = (q + 1, h) if q < 3 else (1, jnp.minimum(h + 1, GROUP - 1))
            peak = jnp.max(top[...], axis=0, keepdims=True)
            if first:
                new = jnp.maximum(peak, FLOOR)
                total = None
            else:
                old = max_in[q, h]
                new = jnp.maximum(old, peak)
                total = acc_in[q, h] * jnp.exp2((old - new) * LOG_SCALE)
            row_max[q, h] = new
            best = None
            here, there = len(parts[q]), len(parts[q_next])
            done = 0
            for at, (n, i) in enumerate(parts[q]):
                until = (at + 1) * there // here
                for other in range(done, until):
                    best = score_into(q_next, h_next, other, best)
                done = until
                weights = jnp.exp2(
                    (scores[q][at * TOK : (at + 1) * TOK, :] - new) * LOG_SCALE
                ).astype(BF16)
                part = dot(v_buf[n, i], weights, ((1,), (0,)))
                total = part if total is None else total + part
            acc[q, h] = total
            top[...] = best
        return carry

    lax.fori_loop(0, GROUP, head, 0)

    if first:
        acc[0] = jnp.zeros((GROUP, VROWS, TOK), F32)
        row_max[0] = jnp.full((GROUP, 1, TOK), FLOOR, F32)
    else:
        acc[0] = acc_in[0]
        row_max[0] = max_in[0]

    def by_number(n, q, i):
        rows = key_block(n, i)[2 * TOK : 2 * TOK + 16, :].astype(F32)
        key_ids = []
        for half in range(2):
            line = rows[half : half + 1, :] * 32.0 + rows[half + 2 : half + 3, :]
            key_ids.append(jnp.broadcast_to(line, (128, 128)).T)
        key_ids = jnp.concatenate(key_ids, axis=0)
        tail = query_block(q)[TOK : TOK + 16, :].astype(F32)
        query_ids = (tail[:, 0:TOK] * 32.0 + tail[:, TOK : 2 * TOK])[0:1, :]
        seen = jnp.concatenate([key_ids, key_ids], axis=1) <= query_ids
        s = score(q, 0, n, i)
        for h in range(GROUP):
            s_next = score(q, h + 1, n, i) if h + 1 < GROUP else None
            s = jnp.where(seen, s, HIDDEN)
            old = row_max[q, h]
            new = jnp.maximum(old, jnp.max(s, axis=0, keepdims=True))
            weights = jnp.exp2((s - new) * LOG_SCALE).astype(BF16)
            acc[q, h] = acc[q, h] * jnp.exp2((old - new) * LOG_SCALE) + dot(
                v_buf[n, i], weights, ((1,), (0,))
            )
            row_max[q, h] = new
            s = s_next

    for n, step in enumerate(steps):
        kind = (z + step + 4) % 4
        count = jnp.minimum((z + 5 - kind) // 4, 4)

        def run(t, carry, n=n):
            q = (t + 4 - d) % 4
            by_number(n, q, q)
            return carry

        lax.fori_loop(0, count, run, 0)
        if step == 1:
            @pl.when((z == NZ - 1) & (y < NY - 1))
            def _(n=n):
                by_number(n, y, y + 1)

    if last:
        for q in range(4):
            sums = []
            for h in range(GROUP):
                total = jnp.maximum(acc[q, h, HEAD : HEAD + 1, :], 0.5)
                out_ref[q, h * HEAD : (h + 1) * HEAD, :] = (
                    acc[q, h, 0:HEAD, :] * (1.0 / total)
                ).astype(BF16)
                sums.append(row_max[q, h] * LOG_SCALE + jnp.log2(total))
            log_sum = jnp.concatenate(sums, axis=0)
            high = log_sum.astype(BF16).astype(F32)
            mid = (log_sum - high).astype(BF16).astype(F32)
            low = log_sum - high - mid
            out_ref[q, GROUP * HEAD : OROWS, :] = jnp.concatenate(
                [high, mid, low, jnp.zeros_like(low)], axis=0
            ).astype(BF16)


def attend(steps, first, last, place, q, blocks, state):
    vmem = pl.BlockSpec(memory_space=pltpu.VMEM)
    n = len(steps)
    acc = jax.ShapeDtypeStruct((4, GROUP, VROWS, TOK), F32)
    row_max = jax.ShapeDtypeStruct((4, GROUP, 1, TOK), F32)
    running = [pltpu.VMEM(acc.shape, F32), pltpu.VMEM(row_max.shape, F32)]
    scores = 10 * n * 4 * TOK * TOK
    return pl.pallas_call(
        functools.partial(attend_kernel, steps, first, last),
        out_shape=jax.ShapeDtypeStruct((4, OROWS, TOK), BF16) if last else (acc, row_max),
        in_specs=[pl.BlockSpec(memory_space=pltpu.SMEM)] * 2
        + [vmem] * (1 + len(blocks) + len(state)),
        out_specs=vmem if last else (vmem, vmem),
        input_output_aliases={} if first or last else {3 + n: 0, 4 + n: 1},
        scratch_shapes=(running if last else [])
        + [
            pltpu.VMEM((n, 4, VROWS, TOK), BF16),
            pltpu.VMEM((n * TOK, TOK), F32),
            pltpu.VMEM((2 * n * TOK, TOK), F32),
            pltpu.VMEM((3 * n * TOK, TOK), F32),
            pltpu.VMEM((8, TOK), F32),
        ],
        compiler_params=pltpu.CompilerParams(vmem_limit_bytes=20 * 2**20),
        cost_estimate=pl.CostEstimate(
            flops=scores * 8 * HEAD, transcendentals=scores, bytes_accessed=6 * 2**20
        ),
        name="attend",
    )(*place, q, *blocks, *state)


def combine_kernel(parts, out_ref):
    logs = []
    for y in range(NY):
        tail = parts[y, GROUP * HEAD : OROWS, :].astype(F32)
        logs.append(tail[0:4] + tail[4:8] + tail[8:12])
    best = functools.reduce(jnp.maximum, logs)
    shares = [jnp.exp2(l - best) for l in logs]
    whole = 1.0 / functools.reduce(jnp.add, shares)
    for h in range(GROUP):
        rows = slice(h * HEAD, (h + 1) * HEAD)
        total = None
        for y in range(NY):
            part = parts[y, rows, :].astype(F32) * (shares[y] * whole)[h : h + 1, :]
            total = part if total is None else total + part
        out_ref[:, rows] = total.T.astype(BF16)


def combine(parts):
    vmem = pl.BlockSpec(memory_space=pltpu.VMEM)
    return pl.pallas_call(
        combine_kernel,
        out_shape=jax.ShapeDtypeStruct((TOK, GROUP * HEAD), BF16),
        in_specs=[vmem],
        out_specs=vmem,
        compiler_params=pltpu.CompilerParams(vmem_limit_bytes=16 * 2**20),
        name="combine",
    )(parts)


def pack_kernel(core, weight, out):
    out[0] = weight[...]


def pack(core, weight):
    return pl.pallas_call(
        pack_kernel,
        grid_spec=pltpu.PrefetchScalarGridSpec(
            num_scalar_prefetch=1,
            grid=(NX,),
            in_specs=[pl.BlockSpec((WIDTH, WIDTH), lambda x, core: (0, 2 * x + 1 - core[0]))],
            out_specs=pl.BlockSpec((1, WIDTH, WIDTH), lambda x, core: (x, 0, 0)),
        ),
        out_shape=jax.ShapeDtypeStruct((NX, WIDTH, WIDTH), BF16),
        compiler_params=pltpu.CompilerParams(vmem_limit_bytes=16 * 2**20),
        name="pack",
    )(core, weight)


def project_kernel(core, both, own_weight, other_weight, out_ref):
    mine, other = both[core[0]], both[1 - core[0]]
    out_ref[0] = (
        dot(mine, own_weight[...], ((1,), (0,))) + dot(other, other_weight[0], ((1,), (0,)))
    ).astype(BF16)


def project(core, both, own_weight, other_weight):
    return pl.pallas_call(
        project_kernel,
        grid_spec=pltpu.PrefetchScalarGridSpec(
            num_scalar_prefetch=1,
            grid=(NX,),
            in_specs=[
                pl.BlockSpec((2, TOK, WIDTH), lambda x, core: (0, 0, 0)),
                pl.BlockSpec((WIDTH, WIDTH), lambda x, core: (0, 2 * x + core[0])),
                pl.BlockSpec((1, WIDTH, WIDTH), lambda x, core: (x, 0, 0)),
            ],
            out_specs=pl.BlockSpec((1, TOK, WIDTH), lambda x, core: (x, 0, 0)),
        ),
        out_shape=jax.ShapeDtypeStruct((NX, TOK, WIDTH), BF16),
        compiler_params=pltpu.CompilerParams(vmem_limit_bytes=16 * 2**20),
        name="project",
    )(core, both, own_weight, other_weight)


def stage_kernel(q, k, v, ids, q_out, block_out):
    high = (ids[...] >> 5).astype(F32)
    low = (ids[...] & 31).astype(F32)
    q_out[0:TOK, :] = q[...]
    terms = (high[0:1], high[1:2], low[0:1], low[1:2])
    for n, term in enumerate(terms):
        q_out[TOK:QROWS, n * 128 : (n + 1) * 128] = jnp.broadcast_to(term, (16, 128)).astype(BF16)
    block_out[0:TOK, :] = k[...]
    block_out[TOK : 2 * TOK, :] = v[...]
    block_out[2 * TOK : ROWS, :] = jnp.concatenate(
        [high, low, jnp.zeros((12, 128), F32)], axis=0
    ).astype(BF16)


def stage(q, k, v, ids):
    vmem = pl.BlockSpec(memory_space=pltpu.VMEM)
    return pl.pallas_call(
        stage_kernel,
        out_shape=(
            jax.ShapeDtypeStruct((QROWS, WIDTH), BF16),
            jax.ShapeDtypeStruct((ROWS, HEAD), BF16),
        ),
        in_specs=[vmem] * 4,
        out_specs=(vmem, vmem),
        compiler_params=pltpu.CompilerParams(vmem_limit_bytes=56 * 2**20),
        name="stage",
    )(q, k, v, ids)


def local(queries, keys, values, block_ids, out_weight):
    ctx = ("y", "z")
    place = [lax.axis_index(axis).reshape(1) for axis in ctx]
    core = lax.axis_index("core").reshape(1)

    staged, block = stage(queries, keys, values, block_ids.reshape(2, 128))
    q_others = [
        lax.ppermute(staged, "y", [((i + n) % NY, i) for i in range(NY)]) for n in (1, 2, 3)
    ]
    own = lax.all_gather(block, ctx, axis=0, axis_index_groups=ring_groups())
    ahead = lax.ppermute(own, ctx, ring_step(1))
    behind = lax.ppermute(own, ctx, ring_step(-1))

    q_all = jnp.stack([staged, *q_others])
    state = attend((0,), True, False, place, q_all, [own], ())
    sent, row_max = lax.optimization_barrier((jnp.where(core == 0, ahead, behind), state[1]))
    state = (state[0], row_max)
    far = lax.ppermute(
        sent,
        (*ctx, "core"),
        [(2 * a + c, 2 * b + c) for c in range(2) for a, b in ring_step(1 - 2 * c)],
    )
    state = attend((1, -1), False, False, place, q_all, [ahead, behind], state)
    partial = attend((2,), False, True, place, q_all, [far], state)
    weight, partial = lax.optimization_barrier((out_weight, partial))
    other_weight = lax.ppermute(pack(core, weight), "core", [(0, 1), (1, 0)])
    partial = lax.all_to_all(partial, "y", 0, 0, tiled=True)
    both = lax.all_gather(combine(partial), "core", axis=0)
    share = project(core, both, out_weight, other_weight)
    shares = lax.all_to_all(share, "x", 0, 0, tiled=True)
    return jnp.sum(shares.astype(F32), axis=0).astype(BF16)


def solution(mesh):
    grid = Mesh(mesh.devices.reshape(NY, NZ, NX, 2), ("y", "z", "x", "core"))
    ctx, head = ("y", "z"), ("x", "core")
    return jax.shard_map(
        local,
        mesh=grid,
        in_specs=(P(ctx, head), P(ctx, head), P(ctx, head), P(ctx), P(head, None)),
        out_specs=P(ctx, head),
        check_vma=False,
    )
```

```python
import functools

import jax
import jax.numpy as jnp
import numpy as np
from jax import lax
from jax.experimental import pallas as pl
from jax.experimental.pallas import tpu as pltpu
from jax.sharding import Mesh
from jax.sharding import PartitionSpec as P

HEAD = 128
GROUP = 4
TOK = 256
LOG_SCALE = float(128**-0.5 * np.log2(np.e))
HIDDEN = -1e30
FLOOR = -1e29
ROWS = TOK * 2 + 16
QROWS = TOK + 16
OROWS = GROUP * HEAD + 16
VROWS = HEAD + 16
WIDTH = GROUP * HEAD
F32, BF16 = jnp.float32, jnp.bfloat16
NX, NY, NZ = 4, 4, 16


def ring_place(d, z):
    return ((z // 4 - d) % NY) * NZ + z


def ring_step(step):
    return [
        (ring_place(d, (z + step) % NZ), ring_place(d, z)) for d in range(4) for z in range(NZ)
    ]


def ring_groups():
    return [
        [i * NZ + ((i + d) % 4) * 4 + zl for i in range(4)] for d in range(4) for zl in range(4)
    ]


def dot(a, b, dims):
    return lax.dot_general(a, b, (dims, ((), ())), preferred_element_type=F32)


def attend_kernel(steps, first, last, y_ref, z_ref, q_ref, *refs):
    kinds = len(steps)
    blocks, refs = refs[:kinds], refs[kinds:]
    y, z = y_ref[0], z_ref[0]
    d = (z // 4 + 4 - y) % 4
    if first:
        acc_in = max_in = None
    else:
        acc_in, max_in, *refs = refs
    if last:
        out_ref, acc, row_max, *refs = refs
    else:
        acc, row_max, *refs = refs
    v_buf, score_1, score_2, score_3, top = refs
    scores = (None, score_1, score_2, score_3)

    def key_block(n, i):
        return blocks[n].at[i]

    def query_block(q):
        return q_ref.at[(q + 4 - y) % 4]

    for n in range(kinds):
        for i in range(4):
            v_buf[n, i, 0:HEAD, :] = key_block(n, i)[TOK : 2 * TOK, :].T
            v_buf[n, i, HEAD:VROWS, :] = jnp.ones((16, TOK), BF16)

    def query(q, h):
        return query_block(q)[0:TOK, pl.ds(pl.multiple_of(h * HEAD, HEAD), HEAD)]

    def score(q, h, n, i):
        return dot(key_block(n, i)[0:TOK, :], query(q, h), ((1,), (1,)))

    def fold(s):
        return jnp.max(s.reshape(TOK // 8, 8, TOK), axis=0)

    parts = [[(n, i) for i in range(q) for n in range(kinds)] for q in range(4)]

    def score_into(q, h, at, best):
        s = score(q, h, *parts[q][at])
        scores[q][at * TOK : (at + 1) * TOK, :] = s
        return fold(s) if best is None else jnp.maximum(best, fold(s))

    best = None
    for at in range(len(parts[1])):
        best = score_into(1, 0, at, best)
    top[...] = best

    def head(h, carry):
        for q in range(1, 4):
            q_next, h_next = (q + 1, h) if q < 3 else (1, jnp.minimum(h + 1, GROUP - 1))
            peak = jnp.max(top[...], axis=0, keepdims=True)
            if first:
                new = jnp.maximum(peak, FLOOR)
                total = None
            else:
                old = max_in[q, h]
                new = jnp.maximum(old, peak)
                total = acc_in[q, h] * jnp.exp2((old - new) * LOG_SCALE)
            row_max[q, h] = new
            best = None
            here, there = len(parts[q]), len(parts[q_next])
            done = 0
            for at, (n, i) in enumerate(parts[q]):
                until = (at + 1) * there // here
                for other in range(done, until):
                    best = score_into(q_next, h_next, other, best)
                done = until
                weights = jnp.exp2(
                    (scores[q][at * TOK : (at + 1) * TOK, :] - new) * LOG_SCALE
                ).astype(BF16)
                part = dot(v_buf[n, i], weights, ((1,), (0,)))
                total = part if total is None else total + part
            acc[q, h] = total
            top[...] = best
        return carry

    lax.fori_loop(0, GROUP, head, 0)

    if first:
        acc[0] = jnp.zeros((GROUP, VROWS, TOK), F32)
        row_max[0] = jnp.full((GROUP, 1, TOK), FLOOR, F32)
    else:
        acc[0] = acc_in[0]
        row_max[0] = max_in[0]

    def by_number(n, q, i):
        rows = key_block(n, i)[2 * TOK : 2 * TOK + 16, :].astype(F32)
        key_ids = []
        for half in range(2):
            line = rows[half : half + 1, :] * 32.0 + rows[half + 2 : half + 3, :]
            key_ids.append(jnp.broadcast_to(line, (128, 128)).T)
        key_ids = jnp.concatenate(key_ids, axis=0)
        tail = query_block(q)[TOK : TOK + 16, :].astype(F32)
        query_ids = (tail[:, 0:TOK] * 32.0 + tail[:, TOK : 2 * TOK])[0:1, :]
        seen = jnp.concatenate([key_ids, key_ids], axis=1) <= query_ids
        s = score(q, 0, n, i)
        for h in range(GROUP):
            s_next = score(q, h + 1, n, i) if h + 1 < GROUP else None
            s = jnp.where(seen, s, HIDDEN)
            old = row_max[q, h]
            new = jnp.maximum(old, jnp.max(s, axis=0, keepdims=True))
            weights = jnp.exp2((s - new) * LOG_SCALE).astype(BF16)
            acc[q, h] = acc[q, h] * jnp.exp2((old - new) * LOG_SCALE) + dot(
                v_buf[n, i], weights, ((1,), (0,))
            )
            row_max[q, h] = new
            s = s_next

    for n, step in enumerate(steps):
        kind = (z + step + 4) % 4
        count = jnp.minimum((z + 5 - kind) // 4, 4)

        def run(t, carry, n=n):
            q = (t + 4 - d) % 4
            by_number(n, q, q)
            return carry

        lax.fori_loop(0, count, run, 0)
        if step == 1:
            @pl.when((z == NZ - 1) & (y < NY - 1))
            def _(n=n):
                by_number(n, y, y + 1)

    if last:
        for q in range(4):
            sums = []
            for h in range(GROUP):
                total = jnp.maximum(acc[q, h, HEAD : HEAD + 1, :], 0.5)
                out_ref[q, h * HEAD : (h + 1) * HEAD, :] = (
                    acc[q, h, 0:HEAD, :] * (1.0 / total)
                ).astype(BF16)
                sums.append(row_max[q, h] * LOG_SCALE + jnp.log2(total))
            log_sum = jnp.concatenate(sums, axis=0)
            high = log_sum.astype(BF16).astype(F32)
            mid = (log_sum - high).astype(BF16).astype(F32)
            low = log_sum - high - mid
            out_ref[q, GROUP * HEAD : OROWS, :] = jnp.concatenate(
                [high, mid, low, jnp.zeros_like(low)], axis=0
            ).astype(BF16)


def attend(steps, first, last, place, q, blocks, state):
    vmem = pl.BlockSpec(memory_space=pltpu.VMEM)
    n = len(steps)
    acc = jax.ShapeDtypeStruct((4, GROUP, VROWS, TOK), F32)
    row_max = jax.ShapeDtypeStruct((4, GROUP, 1, TOK), F32)
    running = [pltpu.VMEM(acc.shape, F32), pltpu.VMEM(row_max.shape, F32)]
    scores = 10 * n * 4 * TOK * TOK
    return pl.pallas_call(
        functools.partial(attend_kernel, steps, first, last),
        out_shape=jax.ShapeDtypeStruct((4, OROWS, TOK), BF16) if last else (acc, row_max),
        in_specs=[pl.BlockSpec(memory_space=pltpu.SMEM)] * 2
        + [vmem] * (1 + len(blocks) + len(state)),
        out_specs=vmem if last else (vmem, vmem),
        input_output_aliases={} if first or last else {3 + n: 0, 4 + n: 1},
        scratch_shapes=(running if last else [])
        + [
            pltpu.VMEM((n, 4, VROWS, TOK), BF16),
            pltpu.VMEM((n * TOK, TOK), F32),
            pltpu.VMEM((2 * n * TOK, TOK), F32),
            pltpu.VMEM((3 * n * TOK, TOK), F32),
            pltpu.VMEM((8, TOK), F32),
        ],
        compiler_params=pltpu.CompilerParams(vmem_limit_bytes=20 * 2**20),
        cost_estimate=pl.CostEstimate(
            flops=scores * 8 * HEAD, transcendentals=scores, bytes_accessed=6 * 2**20
        ),
        name="attend",
    )(*place, q, *blocks, *state)


def combine_kernel(parts, out_ref):
    logs = []
    for y in range(NY):
        tail = parts[y, GROUP * HEAD : OROWS, :].astype(F32)
        logs.append(tail[0:4] + tail[4:8] + tail[8:12])
    best = functools.reduce(jnp.maximum, logs)
    shares = [jnp.exp2(l - best) for l in logs]
    whole = 1.0 / functools.reduce(jnp.add, shares)
    for h in range(GROUP):
        rows = slice(h * HEAD, (h + 1) * HEAD)
        total = None
        for y in range(NY):
            part = parts[y, rows, :].astype(F32) * (shares[y] * whole)[h : h + 1, :]
            total = part if total is None else total + part
        out_ref[:, rows] = total.T.astype(BF16)


def combine(parts):
    vmem = pl.BlockSpec(memory_space=pltpu.VMEM)
    return pl.pallas_call(
        combine_kernel,
        out_shape=jax.ShapeDtypeStruct((TOK, GROUP * HEAD), BF16),
        in_specs=[vmem],
        out_specs=vmem,
        compiler_params=pltpu.CompilerParams(vmem_limit_bytes=16 * 2**20),
        name="combine",
    )(parts)


def pack_kernel(core, weight, out):
    out[0] = weight[...]


def pack(core, weight):
    return pl.pallas_call(
        pack_kernel,
        grid_spec=pltpu.PrefetchScalarGridSpec(
            num_scalar_prefetch=1,
            grid=(NX,),
            in_specs=[pl.BlockSpec((WIDTH, WIDTH), lambda x, core: (0, 2 * x + 1 - core[0]))],
            out_specs=pl.BlockSpec((1, WIDTH, WIDTH), lambda x, core: (x, 0, 0)),
        ),
        out_shape=jax.ShapeDtypeStruct((NX, WIDTH, WIDTH), BF16),
        compiler_params=pltpu.CompilerParams(vmem_limit_bytes=16 * 2**20),
        name="pack",
    )(core, weight)


def project_kernel(core, both, own_weight, other_weight, out_ref):
    mine, other = both[core[0]], both[1 - core[0]]
    out_ref[0] = (
        dot(mine, own_weight[...], ((1,), (0,))) + dot(other, other_weight[0], ((1,), (0,)))
    ).astype(BF16)


def project(core, both, own_weight, other_weight):
    return pl.pallas_call(
        project_kernel,
        grid_spec=pltpu.PrefetchScalarGridSpec(
            num_scalar_prefetch=1,
            grid=(NX,),
            in_specs=[
                pl.BlockSpec((2, TOK, WIDTH), lambda x, core: (0, 0, 0)),
                pl.BlockSpec((WIDTH, WIDTH), lambda x, core: (0, 2 * x + core[0])),
                pl.BlockSpec((1, WIDTH, WIDTH), lambda x, core: (x, 0, 0)),
            ],
            out_specs=pl.BlockSpec((1, TOK, WIDTH), lambda x, core: (x, 0, 0)),
        ),
        out_shape=jax.ShapeDtypeStruct((NX, TOK, WIDTH), BF16),
        compiler_params=pltpu.CompilerParams(vmem_limit_bytes=16 * 2**20),
        name="project",
    )(core, both, own_weight, other_weight)


def stage_kernel(q, k, v, ids, q_out, block_out):
    high = (ids[...] >> 5).astype(F32)
    low = (ids[...] & 31).astype(F32)
    q_out[0:TOK, :] = q[...]
    terms = (high[0:1], high[1:2], low[0:1], low[1:2])
    for n, term in enumerate(terms):
        q_out[TOK:QROWS, n * 128 : (n + 1) * 128] = jnp.broadcast_to(term, (16, 128)).astype(BF16)
    block_out[0:TOK, :] = k[...]
    block_out[TOK : 2 * TOK, :] = v[...]
    block_out[2 * TOK : ROWS, :] = jnp.concatenate(
        [high, low, jnp.zeros((12, 128), F32)], axis=0
    ).astype(BF16)


def stage(q, k, v, ids):
    vmem = pl.BlockSpec(memory_space=pltpu.VMEM)
    return pl.pallas_call(
        stage_kernel,
        out_shape=(
            jax.ShapeDtypeStruct((QROWS, WIDTH), BF16),
            jax.ShapeDtypeStruct((ROWS, HEAD), BF16),
        ),
        in_specs=[vmem] * 4,
        out_specs=(vmem, vmem),
        compiler_params=pltpu.CompilerParams(vmem_limit_bytes=56 * 2**20),
        name="stage",
    )(q, k, v, ids)


def local(queries, keys, values, block_ids, out_weight):
    ctx = ("y", "z")
    place = [lax.axis_index(axis).reshape(1) for axis in ctx]
    core = lax.axis_index("core").reshape(1)

    staged, block = stage(queries, keys, values, block_ids.reshape(2, 128))
    q_others = [
        lax.ppermute(staged, "y", [((i + n) % NY, i) for i in range(NY)]) for n in (1, 2, 3)
    ]
    own = lax.all_gather(block, ctx, axis=0, axis_index_groups=ring_groups())
    behind = lax.ppermute(own, ctx, ring_step(-1))
    ahead = lax.ppermute(own, ctx, ring_step(1))

    q_all = jnp.stack([staged, *q_others])
    state = attend((0,), True, False, place, q_all, [own], ())
    weight, row_max = lax.optimization_barrier((out_weight, state[1]))
    state = (state[0], row_max)
    other_weight = lax.ppermute(pack(core, weight), "core", [(0, 1), (1, 0)])
    far = lax.ppermute(
        jnp.where(core == 1, behind, ahead),
        (*ctx, "core"),
        [(2 * a + c, 2 * b + c) for c in range(2) for a, b in ring_step(1 - 2 * c)],
    )
    state = attend((-1, 1), False, False, place, q_all, [behind, ahead], state)
    partial = attend((2,), False, True, place, q_all, [far], state)
    partial = lax.all_to_all(partial, "y", 0, 0, tiled=True)
    both = lax.all_gather(combine(partial), "core", axis=0)
    share = project(core, both, out_weight, other_weight)
    shares = lax.all_to_all(share, "x", 0, 0, tiled=True)
    return jnp.sum(shares.astype(F32), axis=0).astype(BF16)


def solution(mesh):
    grid = Mesh(mesh.devices.reshape(NY, NZ, NX, 2), ("y", "z", "x", "core"))
    ctx, head = ("y", "z"), ("x", "core")
    return jax.shard_map(
        local,
        mesh=grid,
        in_specs=(P(ctx, head), P(ctx, head), P(ctx, head), P(ctx), P(head, None)),
        out_specs=P(ctx, head),
        check_vma=False,
    )
```

```python
import functools

import jax
import jax.numpy as jnp
import numpy as np
from jax import lax
from jax.experimental import pallas as pl
from jax.experimental.pallas import tpu as pltpu
from jax.sharding import Mesh
from jax.sharding import PartitionSpec as P

HEAD = 128
GROUP = 4
TOK = 256
LOG_SCALE = float(128**-0.5 * np.log2(np.e))
HIDDEN = -1e30
FLOOR = -1e29
ROWS = TOK * 2 + 16
QROWS = TOK + 16
OROWS = GROUP * HEAD + 16
VROWS = HEAD + 16
WIDTH = GROUP * HEAD
F32, BF16 = jnp.float32, jnp.bfloat16
NX, NY, NZ = 4, 4, 16


def ring_place(d, z):
    return ((z // 4 - d) % NY) * NZ + z


def ring_step(step):
    return [
        (ring_place(d, (z + step) % NZ), ring_place(d, z)) for d in range(4) for z in range(NZ)
    ]


def ring_groups():
    return [
        [i * NZ + ((i + d) % 4) * 4 + zl for i in range(4)] for d in range(4) for zl in range(4)
    ]


def dot(a, b, dims):
    return lax.dot_general(a, b, (dims, ((), ())), preferred_element_type=F32)


def attend_kernel(steps, first, last, y_ref, z_ref, q_ref, *refs):
    kinds = len(steps)
    blocks, refs = refs[:kinds], refs[kinds:]
    y, z = y_ref[0], z_ref[0]
    d = (z // 4 + 4 - y) % 4
    if first:
        acc_in = max_in = None
    else:
        acc_in, max_in, *refs = refs
    if last:
        out_ref, acc, row_max, *refs = refs
    else:
        acc, row_max, *refs = refs
    v_buf, score_1, score_2, score_3, top = refs
    scores = (None, score_1, score_2, score_3)

    def key_block(n, i):
        return blocks[n].at[i]

    def query_block(q):
        return q_ref.at[(q + 4 - y) % 4]

    for n in range(kinds):
        for i in range(4):
            v_buf[n, i, 0:HEAD, :] = key_block(n, i)[TOK : 2 * TOK, :].T
            v_buf[n, i, HEAD:VROWS, :] = jnp.ones((16, TOK), BF16)

    def query(q, h):
        return query_block(q)[0:TOK, pl.ds(pl.multiple_of(h * HEAD, HEAD), HEAD)]

    def score(q, h, n, i):
        return dot(key_block(n, i)[0:TOK, :], query(q, h), ((1,), (1,)))

    def fold(s):
        return jnp.max(s.reshape(TOK // 8, 8, TOK), axis=0)

    parts = [[(n, i) for i in range(q) for n in range(kinds)] for q in range(4)]

    def score_into(q, h, at, best):
        s = score(q, h, *parts[q][at])
        scores[q][at * TOK : (at + 1) * TOK, :] = s
        return fold(s) if best is None else jnp.maximum(best, fold(s))

    best = None
    for at in range(len(parts[1])):
        best = score_into(1, 0, at, best)
    top[...] = best

    def head(h, carry):
        for q in range(1, 4):
            q_next, h_next = (q + 1, h) if q < 3 else (1, jnp.minimum(h + 1, GROUP - 1))
            peak = jnp.max(top[...], axis=0, keepdims=True)
            if first:
                new = jnp.maximum(peak, FLOOR)
                total = None
            else:
                old = max_in[q, h]
                new = jnp.maximum(old, peak)
                total = acc_in[q, h] * jnp.exp2((old - new) * LOG_SCALE)
            row_max[q, h] = new
            best = None
            here, there = len(parts[q]), len(parts[q_next])
            done = 0
            for at, (n, i) in enumerate(parts[q]):
                until = (at + 1) * there // here
                for other in range(done, until):
                    best = score_into(q_next, h_next, other, best)
                done = until
                weights = jnp.exp2(
                    (scores[q][at * TOK : (at + 1) * TOK, :] - new) * LOG_SCALE
                ).astype(BF16)
                part = dot(v_buf[n, i], weights, ((1,), (0,)))
                total = part if total is None else total + part
            acc[q, h] = total
            top[...] = best
        return carry

    lax.fori_loop(0, GROUP, head, 0)

    if first:
        acc[0] = jnp.zeros((GROUP, VROWS, TOK), F32)
        row_max[0] = jnp.full((GROUP, 1, TOK), FLOOR, F32)
    else:
        acc[0] = acc_in[0]
        row_max[0] = max_in[0]

    def by_number(n, q, i):
        rows = key_block(n, i)[2 * TOK : 2 * TOK + 16, :].astype(F32)
        key_ids = []
        for half in range(2):
            line = rows[half : half + 1, :] * 32.0 + rows[half + 2 : half + 3, :]
            key_ids.append(jnp.broadcast_to(line, (128, 128)).T)
        key_ids = jnp.concatenate(key_ids, axis=0)
        tail = query_block(q)[TOK : TOK + 16, :].astype(F32)
        query_ids = (tail[:, 0:TOK] * 32.0 + tail[:, TOK : 2 * TOK])[0:1, :]
        seen = jnp.concatenate([key_ids, key_ids], axis=1) <= query_ids
        s = score(q, 0, n, i)
        for h in range(GROUP):
            s_next = score(q, h + 1, n, i) if h + 1 < GROUP else None
            s = jnp.where(seen, s, HIDDEN)
            old = row_max[q, h]
            new = jnp.maximum(old, jnp.max(s, axis=0, keepdims=True))
            weights = jnp.exp2((s - new) * LOG_SCALE).astype(BF16)
            acc[q, h] = acc[q, h] * jnp.exp2((old - new) * LOG_SCALE) + dot(
                v_buf[n, i], weights, ((1,), (0,))
            )
            row_max[q, h] = new
            s = s_next

    for n, step in enumerate(steps):
        kind = (z + step + 4) % 4
        count = jnp.minimum((z + 5 - kind) // 4, 4)

        def run(t, carry, n=n):
            q = (t + 4 - d) % 4
            by_number(n, q, q)
            return carry

        lax.fori_loop(0, count, run, 0)
        if step == 1:
            @pl.when((z == NZ - 1) & (y < NY - 1))
            def _(n=n):
                by_number(n, y, y + 1)

    if last:
        for q in range(4):
            sums = []
            for h in range(GROUP):
                total = jnp.maximum(acc[q, h, HEAD : HEAD + 1, :], 0.5)
                out_ref[q, h * HEAD : (h + 1) * HEAD, :] = (
                    acc[q, h, 0:HEAD, :] * (1.0 / total)
                ).astype(BF16)
                sums.append(row_max[q, h] * LOG_SCALE + jnp.log2(total))
            log_sum = jnp.concatenate(sums, axis=0)
            high = log_sum.astype(BF16).astype(F32)
            mid = (log_sum - high).astype(BF16).astype(F32)
            low = log_sum - high - mid
            out_ref[q, GROUP * HEAD : OROWS, :] = jnp.concatenate(
                [high, mid, low, jnp.zeros_like(low)], axis=0
            ).astype(BF16)


def attend(steps, first, last, place, q, blocks, state):
    vmem = pl.BlockSpec(memory_space=pltpu.VMEM)
    n = len(steps)
    acc = jax.ShapeDtypeStruct((4, GROUP, VROWS, TOK), F32)
    row_max = jax.ShapeDtypeStruct((4, GROUP, 1, TOK), F32)
    running = [pltpu.VMEM(acc.shape, F32), pltpu.VMEM(row_max.shape, F32)]
    scores = 10 * n * 4 * TOK * TOK
    return pl.pallas_call(
        functools.partial(attend_kernel, steps, first, last),
        out_shape=jax.ShapeDtypeStruct((4, OROWS, TOK), BF16) if last else (acc, row_max),
        in_specs=[pl.BlockSpec(memory_space=pltpu.SMEM)] * 2
        + [vmem] * (1 + len(blocks) + len(state)),
        out_specs=vmem if last else (vmem, vmem),
        input_output_aliases={} if first or last else {3 + n: 0, 4 + n: 1},
        scratch_shapes=(running if last else [])
        + [
            pltpu.VMEM((n, 4, VROWS, TOK), BF16),
            pltpu.VMEM((n * TOK, TOK), F32),
            pltpu.VMEM((2 * n * TOK, TOK), F32),
            pltpu.VMEM((3 * n * TOK, TOK), F32),
            pltpu.VMEM((8, TOK), F32),
        ],
        compiler_params=pltpu.CompilerParams(vmem_limit_bytes=20 * 2**20),
        cost_estimate=pl.CostEstimate(
            flops=scores * 8 * HEAD, transcendentals=scores, bytes_accessed=6 * 2**20
        ),
        name="attend",
    )(*place, q, *blocks, *state)


def combine_kernel(parts, out_ref):
    logs = []
    for y in range(NY):
        tail = parts[y, GROUP * HEAD : OROWS, :].astype(F32)
        logs.append(tail[0:4] + tail[4:8] + tail[8:12])
    best = functools.reduce(jnp.maximum, logs)
    shares = [jnp.exp2(l - best) for l in logs]
    whole = 1.0 / functools.reduce(jnp.add, shares)
    for h in range(GROUP):
        rows = slice(h * HEAD, (h + 1) * HEAD)
        total = None
        for y in range(NY):
            part = parts[y, rows, :].astype(F32) * (shares[y] * whole)[h : h + 1, :]
            total = part if total is None else total + part
        out_ref[:, rows] = total.T.astype(BF16)


def combine(parts):
    vmem = pl.BlockSpec(memory_space=pltpu.VMEM)
    return pl.pallas_call(
        combine_kernel,
        out_shape=jax.ShapeDtypeStruct((TOK, GROUP * HEAD), BF16),
        in_specs=[vmem],
        out_specs=vmem,
        compiler_params=pltpu.CompilerParams(vmem_limit_bytes=16 * 2**20),
        name="combine",
    )(parts)


def pack_kernel(core, weight, out):
    out[0] = weight[...]


def pack(core, weight):
    return pl.pallas_call(
        pack_kernel,
        grid_spec=pltpu.PrefetchScalarGridSpec(
            num_scalar_prefetch=1,
            grid=(NX,),
            in_specs=[pl.BlockSpec((WIDTH, WIDTH), lambda x, core: (0, 2 * x + 1 - core[0]))],
            out_specs=pl.BlockSpec((1, WIDTH, WIDTH), lambda x, core: (x, 0, 0)),
        ),
        out_shape=jax.ShapeDtypeStruct((NX, WIDTH, WIDTH), BF16),
        compiler_params=pltpu.CompilerParams(vmem_limit_bytes=16 * 2**20),
        name="pack",
    )(core, weight)


def project_kernel(core, both, own_weight, other_weight, out_ref):
    mine, other = both[core[0]], both[1 - core[0]]
    out_ref[0] = (
        dot(mine, own_weight[...], ((1,), (0,))) + dot(other, other_weight[0], ((1,), (0,)))
    ).astype(BF16)


def project(core, both, own_weight, other_weight):
    return pl.pallas_call(
        project_kernel,
        grid_spec=pltpu.PrefetchScalarGridSpec(
            num_scalar_prefetch=1,
            grid=(NX,),
            in_specs=[
                pl.BlockSpec((2, TOK, WIDTH), lambda x, core: (0, 0, 0)),
                pl.BlockSpec((WIDTH, WIDTH), lambda x, core: (0, 2 * x + core[0])),
                pl.BlockSpec((1, WIDTH, WIDTH), lambda x, core: (x, 0, 0)),
            ],
            out_specs=pl.BlockSpec((1, TOK, WIDTH), lambda x, core: (x, 0, 0)),
        ),
        out_shape=jax.ShapeDtypeStruct((NX, TOK, WIDTH), BF16),
        compiler_params=pltpu.CompilerParams(vmem_limit_bytes=16 * 2**20),
        name="project",
    )(core, both, own_weight, other_weight)


def stage_kernel(q, k, v, ids, q_out, block_out):
    high = (ids[...] >> 5).astype(F32)
    low = (ids[...] & 31).astype(F32)
    q_out[0:TOK, :] = q[...]
    terms = (high[0:1], high[1:2], low[0:1], low[1:2])
    for n, term in enumerate(terms):
        q_out[TOK:QROWS, n * 128 : (n + 1) * 128] = jnp.broadcast_to(term, (16, 128)).astype(BF16)
    block_out[0:TOK, :] = k[...]
    block_out[TOK : 2 * TOK, :] = v[...]
    block_out[2 * TOK : ROWS, :] = jnp.concatenate(
        [high, low, jnp.zeros((12, 128), F32)], axis=0
    ).astype(BF16)


def stage(q, k, v, ids):
    vmem = pl.BlockSpec(memory_space=pltpu.VMEM)
    return pl.pallas_call(
        stage_kernel,
        out_shape=(
            jax.ShapeDtypeStruct((QROWS, WIDTH), BF16),
            jax.ShapeDtypeStruct((ROWS, HEAD), BF16),
        ),
        in_specs=[vmem] * 4,
        out_specs=(vmem, vmem),
        compiler_params=pltpu.CompilerParams(vmem_limit_bytes=56 * 2**20),
        name="stage",
    )(q, k, v, ids)


def local(queries, keys, values, block_ids, out_weight):
    ctx = ("y", "z")
    place = [lax.axis_index(axis).reshape(1) for axis in ctx]
    core = lax.axis_index("core").reshape(1)

    staged, block = stage(queries, keys, values, block_ids.reshape(2, 128))
    q_others = [
        lax.ppermute(staged, "y", [((i + n) % NY, i) for i in range(NY)]) for n in (1, 3, 2)
    ]
    own = lax.all_gather(block, ctx, axis=0, axis_index_groups=ring_groups())
    ahead = lax.ppermute(own, ctx, ring_step(1))
    behind = lax.ppermute(own, ctx, ring_step(-1))

    q_all = jnp.stack([staged, q_others[0], q_others[2], q_others[1]])
    state = attend((0,), True, False, place, q_all, [own], ())
    weight, row_max = lax.optimization_barrier((out_weight, state[1]))
    state = (state[0], row_max)
    other_weight = lax.ppermute(pack(core, weight), "core", [(0, 1), (1, 0)])
    far = lax.ppermute(
        jnp.where(core == 0, ahead, behind),
        (*ctx, "core"),
        [(2 * a + c, 2 * b + c) for c in range(2) for a, b in ring_step(1 - 2 * c)],
    )
    state = attend((1, -1), False, False, place, q_all, [ahead, behind], state)
    partial = attend((2,), False, True, place, q_all, [far], state)
    partial = lax.all_to_all(partial, "y", 0, 0, tiled=True)
    both = lax.all_gather(combine(partial), "core", axis=0)
    share = project(core, both, out_weight, other_weight)
    shares = lax.all_to_all(share, "x", 0, 0, tiled=True)
    return jnp.sum(shares.astype(F32), axis=0).astype(BF16)


def solution(mesh):
    grid = Mesh(mesh.devices.reshape(NY, NZ, NX, 2), ("y", "z", "x", "core"))
    ctx, head = ("y", "z"), ("x", "core")
    return jax.shard_map(
        local,
        mesh=grid,
        in_specs=(P(ctx, head), P(ctx, head), P(ctx, head), P(ctx), P(head, None)),
        out_specs=P(ctx, head),
        check_vma=False,
    )
```
